256 devices in a mesh: dp: 16 (over z_lo, x), shard: 16 (over y, z_hi, core).
Axes of the slice: x: 4, y: 4, z: 8 (z_hi: 2, z_lo: 4; z = z_hi * 4 + z_lo), core: 2. Of those that a mesh axis runs over, the one named last changes fastest.
Arguments:
- tokens: bfloat16 [32768, 5120], P(('dp', 'shard')), may hold values from -6 to 6
- targets: bfloat16 [2560, 32768], P(None, ('dp', 'shard')), may hold values from -6 to 6
- weight: bfloat16 [2560, 5120], P('shard'), may hold values from -0.078125 to 0.078125
- lanczos_cur: float32 [2560, 5120], P('shard'), may hold values from -60 to 60
- lanczos_prev: float32 [2560, 5120], P('shard'), may hold values from -60 to 60
- beta_prev: float32 [1], replicated, may hold values from 0.5 to 2
Outputs:
- lanczos_next: float32 [2560, 5120], P('shard')
- coefficients: float32 [2], replicated
The draws below stay inside these ranges and needn't reach their ends.
All inputs are finite; a program needn't handle non-finite values.
Results may differ from the reference program's by a relative error of at most 0.0011.
Values may be sent and summed in bfloat16 or wider, within the bound.
No kernel may reach another device: no remote copies, remote signals or barrier semaphores. Data moves between devices by JAX's collectives and lax.ppermute only.
A program may use at most 192 MiB of HBM per device.

```python
import jax
import jax.numpy as jnp
from jax import lax

D = 5120
E = 2560
TOKENS = 32768


def rising_scale():
    rows = jnp.arange(E, dtype=jnp.float32) / jnp.float32(max(E - 1, 1))
    cols = jnp.arange(D, dtype=jnp.float32) / jnp.float32(max(D - 1, 1))
    row_part = jnp.power(jnp.float32(10.0), rows - 0.5)
    col_part = jnp.power(jnp.float32(10.0), cols - 0.5)
    return row_part[:, None] * col_part[None, :]


def vector_draw(key):
    base = jax.random.truncated_normal(key, -4.0, 4.0, (E, D), jnp.float32)
    return base * rising_scale()


def draw_lanczos_cur(key, part):
    key = jax.random.fold_in(key, 11)
    return vector_draw(key)


def draw_lanczos_prev(key, part):
    key = jax.random.fold_in(key, 23)
    return vector_draw(key)


def steps_of(own_key, shape, pieces, least, high):
    def one(axis_at, shards_of):
        draws = jax.random.uniform(jax.random.fold_in(jax.random.fold_in(own_key, 6), axis_at), (shards_of,), jnp.float32, least / len(pieces), high / len(pieces))
        return jnp.repeat(jnp.exp(draws), shape[axis_at] // shards_of).reshape((-1,) + (1,) * (len(shape) - axis_at - 1))

    gain = one(*pieces[0])
    for cut in pieces[1:]:
        gain = gain * one(*cut)
    return gain


def scatter_about(key, shape, scale, reach, cuts=(), kind=jnp.bfloat16):
    loudness = steps_of(key, shape, cuts, -0.22, 0.18) if cuts else 1.0
    values = jax.random.normal(key, shape, jnp.float32) * scale * loudness
    return jnp.minimum(jnp.maximum(values, -reach), reach).astype(kind)


def setup_inputs(seed: int = 0) -> dict:
    keys = jax.random.split(jax.random.key(seed), 7)
    return {
        "tokens": scatter_about(keys[0], (TOKENS, D), 1.0, 6.0, ((0, 256),)),
        "targets": scatter_about(keys[1], (E, TOKENS), 1.0, 6.0, ((1, 256),)),
        "weight": scatter_about(keys[2], (E, D), D ** -0.5, 0.078125, ((0, 16),)),
        "lanczos_cur": draw_lanczos_cur(jax.random.fold_in(keys[6], 71), 0),
        "lanczos_prev": draw_lanczos_prev(jax.random.fold_in(keys[6], 71), 0),
        "beta_prev": jnp.clip(jax.random.uniform(keys[5], (1,), jnp.float32, 0.5, 2.0), 0.5, 2.0),
    }


EPS_NORM = 1e-05
EPS_MEAN = 1e-06

def silu_terms(normed):
    sig = jax.nn.sigmoid(normed)
    first = sig * (1.0 + normed * (1.0 - sig))
    second = sig * (1.0 - sig) * (2.0 + normed * (1.0 - 2.0 * sig))
    return (sig, first, second)

def curvature(hidden, tangent, target, width, count):
    squares = lax.optimization_barrier(jnp.sum(hidden * hidden, 0))
    cross = lax.optimization_barrier(jnp.sum(hidden * tangent, 0))
    scale = lax.rsqrt(squares / width + EPS_NORM)
    scale_dot = -(scale * scale * scale) * cross / width
    normed = hidden * scale
    normed_dot = tangent * scale + hidden * scale_dot
    sig, first, second = silu_terms(normed)
    error = normed * sig - target.astype(jnp.float32)
    grad_u = error * first / count
    grad_dot = (first * first + error * second) * normed_dot / count
    inner = lax.optimization_barrier(jnp.sum(grad_u * hidden, 0)) / width
    inner_dot = lax.optimization_barrier(jnp.sum(grad_dot * hidden + grad_u * tangent, 0)) / width
    cube = scale * scale * scale
    result = scale_dot * grad_u + scale * grad_dot - 3.0 * scale * scale * scale_dot * hidden * inner - cube * tangent * inner - cube * hidden * inner_dot
    return result.astype(jnp.bfloat16)

def reference(tokens, targets, weight, lanczos_cur, lanczos_prev, beta_prev):
    direction = lanczos_cur.astype(jnp.bfloat16)
    flipped = tokens.T
    hidden = jnp.dot(weight, flipped, preferred_element_type=jnp.float32)
    tangent = jnp.dot(direction, flipped, preferred_element_type=jnp.float32)
    curv = curvature(hidden, tangent, targets, jnp.float32(E), jnp.float32(TOKENS))
    product = jnp.dot(curv, tokens, preferred_element_type=jnp.float32)
    entries = jnp.float32(E * D)
    alpha = jnp.sum(lanczos_cur * product) / entries
    resid = product - alpha * lanczos_cur - beta_prev[0] * lanczos_prev
    beta = jnp.sqrt(jnp.sum(resid * resid) / entries + EPS_MEAN)
    return (resid / beta, jnp.stack([alpha, beta]))
```

```python
import jax
import jax.numpy as jnp
from jax import lax
from jax.sharding import Mesh, PartitionSpec as P

EPS_NORM = 1e-05
EPS_MEAN = 1e-06
TOKEN_MAX = 6.0
HALF_MAX = 32000.0
Z = ("zl", "zh")


def place(z):
    return (z % 4) * 2 + z // 4


def shift(n, k):
    return [(i, (i + k) % n) for i in range(n)]


def zshift(k):
    return [(place(i), place((i + k) % 8)) for i in range(8)]


def xor(n, k):
    return [(i, i ^ k) for i in range(n)]


def sum_group(v):
    v = v + lax.ppermute(v, "c", xor(2, 1))
    v = v + lax.ppermute(v, "y", xor(4, 1))
    return v + lax.ppermute(v, "y", xor(4, 3))


def silu_terms(normed):
    sig = jax.nn.sigmoid(normed)
    first = sig * (1.0 + normed * (1.0 - sig))
    second = sig * (1.0 - sig) * (2.0 + normed * (1.0 - 2.0 * sig))
    return (sig, first, second)


def curvature(hidden, tangent, target, width, count):
    sums = sum_group(jnp.stack([jnp.sum(hidden * hidden, 0), jnp.sum(hidden * tangent, 0)]))
    squares, cross = sums[0], sums[1]
    scale = lax.rsqrt(squares / width + EPS_NORM)
    scale_dot = -(scale * scale * scale) * cross / width
    normed = hidden * scale
    normed_dot = tangent * scale + hidden * scale_dot
    sig, first, second = silu_terms(normed)
    error = normed * sig - target.astype(jnp.float32)
    grad_u = error * first / count
    grad_dot = (first * first + error * second) * normed_dot / count
    sums = sum_group(
        jnp.stack([jnp.sum(grad_u * hidden, 0), jnp.sum(grad_dot * hidden + grad_u * tangent, 0)])
    )
    inner = sums[0] / width
    inner_dot = sums[1] / width
    cube = scale * scale * scale
    result = (
        scale_dot * grad_u
        + scale * grad_dot
        - 3.0 * scale * scale * scale_dot * hidden * inner
        - cube * tangent * inner
        - cube * hidden * inner_dot
    )
    return result.astype(jnp.bfloat16)


def take(stack, index):
    return lax.dynamic_index_in_dim(stack, index, 0, keepdims=False)


def other_half(own, x):
    quarters = own.reshape(4, own.shape[0] // 4, own.shape[1])
    part = lax.ppermute(take(quarters, x), "zh", xor(2, 1))
    out = jnp.zeros_like(quarters)
    out = lax.dynamic_update_index_in_dim(out, part, x, 0)
    for k in (1, 3, 2):
        got = lax.ppermute(part, "x", shift(4, k))
        out = lax.dynamic_update_index_in_dim(out, got, (x - k) % 4, 0)
    return out.reshape(own.shape)


def per_device(tokens, targets, weight, cur, prev, beta_prev):
    x, zl, zh = (lax.axis_index(n) for n in ("x", "zl", "zh"))
    z = zh * 4 + zl
    width, own = targets.shape
    rows, depth = weight.shape
    total = own * 256
    f32 = jnp.float32

    gathered = lax.all_gather(tokens, ("y", "c"), axis=0, tiled=True)
    blocks = targets.reshape(4, 2, 2, rows, own).transpose(0, 2, 1, 3, 4).reshape(8, 2 * rows, own)
    columns = lax.all_to_all(blocks, ("y", "c"), split_axis=0, concat_axis=2, tiled=True)
    columns = columns.reshape(2 * rows, 8 * own)

    mine = jnp.concatenate([weight, cur.astype(jnp.bfloat16)])
    other = other_half(mine, x)
    low, high = jnp.where(zh == 0, mine, other), jnp.where(zh == 0, other, mine)
    left = jnp.concatenate([low[:rows], high[:rows], low[rows:], high[rows:]])
    both = lax.dot_general(left, gathered, (((1,), (1,)), ((), ())), preferred_element_type=f32)
    curv = curvature(both[: 2 * rows], both[2 * rows :], columns, f32(width), f32(total))

    bound = jnp.max(jnp.sum(jnp.abs(curv.astype(f32)), 1)) * TOKEN_MAX + 1e-30
    partial = jnp.dot(curv, gathered, preferred_element_type=f32)
    high_rows, wide = rows // 2, depth // 8
    pieces = partial.reshape(2, 2, high_rows, 4, 2, wide).transpose(3, 0, 1, 4, 2, 5)
    pieces = pieces.reshape(4, 8, high_rows, wide)

    packed = (pieces * (HALF_MAX / bound)).astype(jnp.float16)
    share = take(pieces, x)
    tiny = jnp.full((8, 128), bound / HALF_MAX, f32)
    for k in (1, 3, 2):
        got = lax.ppermute(take(packed, (x + k) % 4), "x", shift(4, k))
        unit = lax.ppermute(tiny, "x", shift(4, k))[0, 0]
        share = share + got.astype(f32) * unit
    top = jnp.full((8, 128), bound, f32)
    for k in (1, 3):
        top = jnp.maximum(top, lax.ppermute(top, "x", xor(4, k)))
    for k in (1, 2, 4):
        perm = [(place(i), place(i ^ k)) for i in range(8)]
        top = jnp.maximum(top, lax.ppermute(top, Z, perm))
    top = top[0, 0] * 32.0
    unit, inverse = top / HALF_MAX, HALF_MAX / top

    packed = (share * inverse).astype(jnp.float16)
    piece = take(share, z)
    for k in (1, 7, 2, 6, 3, 5, 4):
        got = lax.ppermute(take(packed, (z + k) % 8), Z, zshift(k))
        piece = piece + got.astype(f32) * unit

    coeff = beta_prev[0]
    spot = ((zl // 2) * high_rows, x * 2 * wide + (zl % 2) * wide)
    c = lax.dynamic_slice(cur, spot, (high_rows, wide))
    q = lax.dynamic_slice(prev, spot, (high_rows, wide))
    w = piece - coeff * q
    dot_cp = jnp.sum(c * piece)
    dot_cc = jnp.sum(c * c)
    best = jnp.sum(w * c) / jnp.maximum(dot_cc, 1e-30)
    least = jnp.sum(jnp.square(w - best * c))
    me = (z * 4 + x) * 8 + lax.axis_index("y") * 2 + lax.axis_index("c")
    table = jnp.stack([dot_cp, dot_cc, best, least])[:, None]
    table = jnp.where(jnp.arange(256)[None, :] == me, table, 0.0)
    table = sum_group(table)
    moved = [lax.ppermute(table, "x", shift(4, k)) for k in (1, 3, 2)]
    table = table + moved[0] + moved[1] + moved[2]
    moved = [lax.ppermute(table, Z, zshift(k)) for k in range(1, 8)]
    for m in moved:
        table = table + m
    entries = f32(width * depth)
    alpha = jnp.sum(table[0]) / entries
    mean_sq = jnp.sum(table[3] + jnp.square(alpha - table[2]) * table[1]) / entries
    beta = jnp.sqrt(mean_sq + EPS_MEAN)

    packed = (piece * inverse).astype(jnp.float16)
    line = jnp.zeros((4, high_rows, wide), jnp.float16)
    line = lax.dynamic_update_index_in_dim(line, packed, zl, 0)
    for k in (1, 3, 2):
        got = lax.ppermute(packed, "zl", shift(4, k))
        line = lax.dynamic_update_index_in_dim(line, got, (zl - k) % 4, 0)
    whole = jnp.zeros((4, 4, high_rows, wide), jnp.float16)
    whole = lax.dynamic_update_index_in_dim(whole, line, x, 0)
    for k in (1, 3, 2):
        got = lax.ppermute(line, "x", shift(4, k))
        whole = lax.dynamic_update_index_in_dim(whole, got, (x - k) % 4, 0)
    product = whole.reshape(4, 2, 2, high_rows, wide).transpose(1, 3, 0, 2, 4).reshape(rows, depth)
    product = product.astype(f32) * unit
    fresh = (product - alpha * cur - coeff * prev) / beta
    return (fresh, jnp.stack([alpha, beta]))


def solution(mesh):
    inner = Mesh(mesh.devices.reshape(4, 4, 4, 2, 2), ("zl", "x", "y", "zh", "c"))
    dp, shard = ("zl", "x"), ("y", "zh", "c")
    return jax.shard_map(
        per_device,
        mesh=inner,
        in_specs=(
            P(dp + shard, None),
            P(None, dp + shard),
            P(shard, None),
            P(shard, None),
            P(shard, None),
            P(),
        ),
        out_specs=(P(shard, None), P()),
        check_vma=False,
    )
```

```python
import jax
import jax.numpy as jnp
from jax import lax
from jax.sharding import Mesh, PartitionSpec as P

EPS_NORM = 1e-05
EPS_MEAN = 1e-06
TOKEN_MAX = 6.0
HALF_BITS = 14.0
Z = ("zl", "zh")


def place(z):
    return (z % 4) * 2 + z // 4


def shift(n, k):
    return [(i, (i + k) % n) for i in range(n)]


def zshift(k):
    return [(place(i), place((i + k) % 8)) for i in range(8)]


def xor(n, k):
    return [(i, i ^ k) for i in range(n)]


def sum_group(v):
    v = v + lax.ppermute(v, "c", xor(2, 1))
    v = v + lax.ppermute(v, "y", xor(4, 1))
    return v + lax.ppermute(v, "y", xor(4, 3))


def silu_terms(normed):
    sig = jax.nn.sigmoid(normed)
    first = sig * (1.0 + normed * (1.0 - sig))
    second = sig * (1.0 - sig) * (2.0 + normed * (1.0 - 2.0 * sig))
    return (sig, first, second)


def curvature(hidden, tangent, target, width, count):
    sums = sum_group(jnp.stack([jnp.sum(hidden * hidden, 0), jnp.sum(hidden * tangent, 0)]))
    squares, cross = sums[0], sums[1]
    scale = lax.rsqrt(squares / width + EPS_NORM)
    scale_dot = -(scale * scale * scale) * cross / width
    normed = hidden * scale
    normed_dot = tangent * scale + hidden * scale_dot
    sig, first, second = silu_terms(normed)
    error = normed * sig - target.astype(jnp.float32)
    grad_u = error * first / count
    grad_dot = (first * first + error * second) * normed_dot / count
    sums = sum_group(
        jnp.stack([jnp.sum(grad_u * hidden, 0), jnp.sum(grad_dot * hidden + grad_u * tangent, 0)])
    )
    inner = sums[0] / width
    inner_dot = sums[1] / width
    cube = scale * scale * scale
    result = (
        scale_dot * grad_u
        + scale * grad_dot
        - 3.0 * scale * scale * scale_dot * hidden * inner
        - cube * tangent * inner
        - cube * hidden * inner_dot
    )
    return result.astype(jnp.bfloat16)


def take(stack, index):
    return lax.dynamic_index_in_dim(stack, index, 0, keepdims=False)


def other_half(own, x):
    quarters = own.reshape(4, own.shape[0] // 4, own.shape[1])
    part = lax.ppermute(take(quarters, x), "zh", xor(2, 1))
    out = jnp.zeros_like(quarters)
    out = lax.dynamic_update_index_in_dim(out, part, x, 0)
    for k in (1, 3, 2):
        got = lax.ppermute(part, "x", shift(4, k))
        out = lax.dynamic_update_index_in_dim(out, got, (x - k) % 4, 0)
    return out.reshape(own.shape)


def per_device(tokens, targets, weight, cur, prev, beta_prev):
    x, zl, zh = (lax.axis_index(n) for n in ("x", "zl", "zh"))
    z = zh * 4 + zl
    width, own = targets.shape
    rows, depth = weight.shape
    total = own * 256
    f32 = jnp.float32

    gathered = lax.all_gather(tokens, ("y", "c"), axis=0, tiled=True)
    blocks = targets.reshape(4, 2, 2, rows, own).transpose(0, 2, 1, 3, 4).reshape(8, 2 * rows, own)
    columns = lax.all_to_all(blocks, ("y", "c"), split_axis=0, concat_axis=2, tiled=True)
    columns = columns.reshape(2 * rows, 8 * own)

    def project(mine):
        other = other_half(mine, x)
        left = jnp.concatenate([jnp.where(zh == 0, mine, other), jnp.where(zh == 0, other, mine)])
        return lax.dot_general(left, gathered, (((1,), (1,)), ((), ())), preferred_element_type=f32)

    hidden = project(weight)
    tangent = project(cur.astype(jnp.bfloat16))
    curv = curvature(hidden, tangent, columns, f32(width), f32(total))

    coeff = beta_prev[0]
    bound = jnp.max(jnp.sum(jnp.abs(curv.astype(f32)), 1)) * TOKEN_MAX
    power = jnp.clip(jnp.ceil(jnp.log2(bound)) + 1.0, -100.0, 100.0)

    quarter = depth // 4
    parts = {}
    for k in (2, 1, 3, 0):
        columns_k = lax.dynamic_slice_in_dim(gathered, ((x + k) % 4) * quarter, quarter, 1)
        part = jnp.dot(curv, columns_k, preferred_element_type=f32)
        if k:
            tail = jnp.full((16, quarter), power, f32).astype(jnp.float16)
            part = jnp.concatenate([(part * jnp.exp2(HALF_BITS - power)).astype(jnp.float16), tail])
            parts[k] = lax.ppermute(part, "x", shift(4, k))
        else:
            share = part
    powers = [power]
    for k in (1, 3, 2):
        got = parts[k]
        powers.append(got[2 * rows, 0].astype(f32))
        share = share + got[: 2 * rows].astype(f32) * jnp.exp2(powers[-1] - HALF_BITS)
    power = jnp.max(jnp.stack(powers)) + 2.0

    share = share.reshape(8, rows // 4, quarter)
    packed = (share * jnp.exp2(HALF_BITS - power)).astype(jnp.float16)
    tail = jnp.full((8, rows // 4, 128), power, f32).astype(jnp.float16)
    packed = jnp.concatenate([packed, tail], 2)
    piece = take(share, z)
    powers = [power]
    for k in (4, 3, 5, 2, 6, 1, 7):
        got = lax.ppermute(take(packed, (z + k) % 8), Z, zshift(k))
        powers.append(got[0, quarter].astype(f32))
        piece = piece + got[:, :quarter].astype(f32) * jnp.exp2(powers[-1] - HALF_BITS)
    power = jnp.max(jnp.stack(powers)) + 3.0
    unit = jnp.exp2(power - HALF_BITS)

    packed = (piece * jnp.exp2(HALF_BITS - power)).astype(jnp.float16)
    line = jnp.zeros((4,) + packed.shape, jnp.float16)
    line = lax.dynamic_update_index_in_dim(line, packed, zl, 0)
    for k in (3, 1, 2):
        got = lax.ppermute(packed, "zl", shift(4, k))
        line = lax.dynamic_update_index_in_dim(line, got, (zl - k) % 4, 0)
    spot = (zl * (rows // 4), x * quarter)
    c = lax.dynamic_slice(cur, spot, packed.shape)
    w = piece - coeff * lax.dynamic_slice(prev, spot, packed.shape)
    dot_cc = jnp.sum(c * c)
    near = jnp.sum(w * c) / jnp.maximum(dot_cc, 1e-30)
    away = w - near * c
    table = [jnp.sum(c * piece), dot_cc, near, jnp.sum(away * away), jnp.sum(away * c)]
    me = (z * 4 + x) * 8 + lax.axis_index("y") * 2 + lax.axis_index("c")
    table = jnp.stack(table + [jnp.zeros((), f32)] * 3)[:, None]
    table = jnp.where(jnp.arange(256)[None, :] == me, table, 0.0)
    table = sum_group(table)
    table = table + lax.ppermute(table, "x", xor(4, 1))
    table = table + lax.ppermute(table, "x", xor(4, 3))

    line = line.reshape(rows, quarter)
    line, table = lax.optimization_barrier((line, table))
    product = jnp.zeros((rows, depth), jnp.float16)
    product = lax.dynamic_update_slice(product, line, (0, x * quarter))
    for k in (2, 1, 3):
        got = lax.ppermute(line, "x", shift(4, k))
        product = lax.dynamic_update_slice(product, got, (0, ((x - k) % 4) * quarter))
    for k in (1, 2, 4):
        table = table + lax.ppermute(table, Z, [(place(i), place(i ^ k)) for i in range(8)])
    entries = f32(16 * rows * depth)
    alpha = jnp.sum(table[0]) / entries
    gap = alpha - table[2]
    mean_sq = jnp.sum(table[3] - 2.0 * gap * table[4] + gap * gap * table[1]) / entries
    beta = jnp.sqrt(jnp.maximum(mean_sq, 0.0) + EPS_MEAN)
    fresh = (product.astype(f32) * unit - alpha * cur - coeff * prev) / beta
    return (fresh, jnp.stack([alpha, beta]))


def solution(mesh):
    inner = Mesh(mesh.devices.reshape(4, 4, 4, 2, 2), ("zl", "x", "y", "zh", "c"))
    dp, shard = ("zl", "x"), ("y", "zh", "c")
    return jax.shard_map(
        per_device,
        mesh=inner,
        in_specs=(
            P(dp + shard, None),
            P(None, dp + shard),
            P(shard, None),
            P(shard, None),
            P(shard, None),
            P(),
        ),
        out_specs=(P(shard, None), P()),
        check_vma=False,
    )
```

```python
import jax
import jax.numpy as jnp
from jax import lax
from jax.experimental import pallas as pl
from jax.experimental.pallas import tpu as pltpu
from jax.sharding import Mesh, PartitionSpec as P

EPS_NORM = 1e-05
EPS_MEAN = 1e-06
PRODUCT_BOUND = 6.0 * 170.0
HALF_BITS = 15.0
Z = ("zl", "zh")
F32 = jnp.float32


def place(z):
    return (z % 4) * 2 + z // 4


def shift(n, k):
    return [(i, (i + k) % n) for i in range(n)]


def zshift(k):
    return [(place(i), place((i + k) % 8)) for i in range(8)]


def xor(n, k):
    return [(i, i ^ k) for i in range(n)]


def sum_group(v):
    v = v + lax.ppermute(v, "c", xor(2, 1))
    v = v + lax.ppermute(v, "y", xor(4, 1))
    return v + lax.ppermute(v, "y", xor(4, 3))


def sum_z(v):
    for k in (1, 2, 4):
        v = v + lax.ppermute(v, Z, [(place(i), place(i ^ k)) for i in range(8)])
    return v


def sum_x(v):
    v = v + lax.ppermute(v, "x", xor(4, 1))
    return v + lax.ppermute(v, "x", xor(4, 3))


def silu_terms(normed):
    sig = jax.nn.sigmoid(normed)
    first = sig * (1.0 + normed * (1.0 - sig))
    second = sig * (1.0 - sig) * (2.0 + normed * (1.0 - 2.0 * sig))
    return (sig, first, second)


def project_kernel(half, tok, w_own, w_other, d_own, d_other, hid, tan, sums, left):
    rows = w_own.shape[0]

    @pl.when(pl.program_id(0) == 0)
    def _():
        own = pl.multiple_of(half[0] * rows, 16)
        other = pl.multiple_of((1 - half[0]) * rows, 16)
        left[pl.ds(own, rows), :] = w_own[...]
        left[pl.ds(other, rows), :] = w_other[...]
        left[pl.ds(2 * rows + own, rows), :] = d_own[...]
        left[pl.ds(2 * rows + other, rows), :] = d_other[...]

    both = lax.dot_general(
        left[...], tok[...], (((1,), (1,)), ((), ())), preferred_element_type=F32
    )
    h, t = both[: 2 * rows], both[2 * rows :]
    hid[...] = h
    tan[...] = t
    sums[...] = jnp.zeros_like(sums)
    sums[0:1, :] = jnp.sum(h * h, 0, keepdims=True)
    sums[1:2, :] = jnp.sum(h * t, 0, keepdims=True)
    sums[2:3, :] = jnp.sum(t * t, 0, keepdims=True)


def project(half, gathered, w_own, w_other, d_own, d_other):
    rows, depth = w_own.shape
    count = gathered.shape[0]
    step = 256
    held = pl.BlockSpec((rows, depth), lambda i, h: (0, 0))
    out = pl.BlockSpec((2 * rows, step), lambda i, h: (0, i))
    return pl.pallas_call(
        project_kernel,
        out_shape=[
            jax.ShapeDtypeStruct((2 * rows, count), F32),
            jax.ShapeDtypeStruct((2 * rows, count), F32),
            jax.ShapeDtypeStruct((8, count), F32),
        ],
        grid_spec=pltpu.PrefetchScalarGridSpec(
            num_scalar_prefetch=1,
            grid=(count // step,),
            in_specs=[pl.BlockSpec((step, depth), lambda i, h: (i, 0)), held, held, held, held],
            out_specs=[out, out, pl.BlockSpec((8, step), lambda i, h: (0, i))],
            scratch_shapes=[pltpu.VMEM((4 * rows, depth), jnp.bfloat16)],
        ),
        compiler_params=pltpu.CompilerParams(vmem_limit_bytes=50 * 2**20),
        cost_estimate=pl.CostEstimate(
            flops=8 * rows * depth * count, bytes_accessed=2 * depth * (count + 4 * rows), transcendentals=0
        ),
    )(half, gathered, w_own, w_other, d_own, d_other)


def table_kernel(where, scalars, piece, cur, prev, out):
    unit, coeff = scalars[0], scalars[1]
    p, c = piece[...] * unit, cur[...]
    w = p - coeff * prev[...]
    dot_cc = jnp.sum(c * c)
    near = jnp.sum(w * c) / jnp.maximum(dot_cc, 1e-30)
    away = w - near * c
    rows = lax.broadcasted_iota(jnp.int32, out.shape, 0)
    values = (jnp.sum(c * p), dot_cc, near, jnp.sum(away * away), jnp.sum(away * c))
    table = jnp.zeros(out.shape, F32)
    for i, v in enumerate(values):
        table = jnp.where(rows == i, v, table)
    out[...] = jnp.where(lax.broadcasted_iota(jnp.int32, out.shape, 1) == where[0], table, 0.0)


def table_of(where, scalars, piece, cur, prev):
    at = pl.BlockSpec(piece.shape, lambda i, w: (w[1], w[2]))
    return pl.pallas_call(
        table_kernel,
        out_shape=jax.ShapeDtypeStruct((8, 256), F32),
        grid_spec=pltpu.PrefetchScalarGridSpec(
            num_scalar_prefetch=1,
            grid=(1,),
            in_specs=[
                pl.BlockSpec(memory_space=pltpu.SMEM),
                pl.BlockSpec(piece.shape, lambda i, w: (0, 0)),
                at,
                at,
            ],
            out_specs=pl.BlockSpec((8, 256), lambda i, w: (0, 0)),
        ),
    )(where, scalars, piece, cur, prev)


def curvature(hidden, tangent, sums, target, width, count):
    sums = sum_group(sums)
    squares, cross = sums[0], sums[1]
    scale = lax.rsqrt(squares / width + EPS_NORM)
    bound = jnp.sum(scale * scale * jnp.sqrt(sums[2])) * (PRODUCT_BOUND / count)
    bound = sum_z(sum_x(jnp.full((8, 128), bound, F32)))[0, 0]
    power = jnp.clip(HALF_BITS - jnp.ceil(jnp.log2(bound)), -100.0, 100.0)
    scale_dot = -(scale * scale * scale) * cross / width
    normed = hidden * scale
    normed_dot = tangent * scale + hidden * scale_dot
    sig, first, second = silu_terms(normed)
    error = normed * sig - target.astype(F32)
    grad_u = error * first / count
    grad_dot = (first * first + error * second) * normed_dot / count
    sums = sum_group(
        jnp.stack([jnp.sum(grad_u * hidden, 0), jnp.sum(grad_dot * hidden + grad_u * tangent, 0)])
    )
    inner = sums[0] / width
    inner_dot = sums[1] / width
    cube = scale * scale * scale
    result = (
        scale_dot * grad_u
        + scale * grad_dot
        - 3.0 * scale * scale * scale_dot * hidden * inner
        - cube * tangent * inner
        - cube * hidden * inner_dot
    )
    return (result * jnp.exp2(power)).astype(jnp.bfloat16), jnp.exp2(-power)


def take(stack, index):
    return lax.dynamic_index_in_dim(stack, index, 0, keepdims=False)


def other_half(own, x):
    quarters = own.reshape(4, own.shape[0] // 4, own.shape[1])
    part = lax.ppermute(take(quarters, x), "zh", xor(2, 1))
    out = jnp.zeros_like(quarters)
    out = lax.dynamic_update_index_in_dim(out, part, x, 0)
    for k in (1, 3, 2):
        got = lax.ppermute(part, "x", shift(4, k))
        out = lax.dynamic_update_index_in_dim(out, got, (x - k) % 4, 0)
    return out.reshape(own.shape)


def per_device(tokens, targets, weight, cur, prev, beta_prev):
    x, zl, zh = (lax.axis_index(n) for n in ("x", "zl", "zh"))
    z = zh * 4 + zl
    width, own = targets.shape
    rows, depth = weight.shape
    total = own * 256

    gathered = lax.all_gather(tokens, ("y", "c"), axis=0, tiled=True)
    blocks = targets.reshape(4, 2, 2, rows, own).transpose(0, 2, 1, 3, 4).reshape(8, 2 * rows, own)
    columns = lax.all_to_all(blocks, ("y", "c"), split_axis=0, concat_axis=2, tiled=True)
    columns = columns.reshape(2 * rows, 8 * own)

    direction = cur.astype(jnp.bfloat16)
    hidden, tangent, sums = project(
        zh[None], gathered, weight, other_half(weight, x), direction, other_half(direction, x)
    )
    curv, unit = curvature(hidden, tangent, sums, columns, F32(width), F32(total))

    quarter = depth // 4
    parts = {}
    for k in (2, 1, 3, 0):
        columns_k = lax.dynamic_slice_in_dim(gathered, ((x + k) % 4) * quarter, quarter, 1)
        part = jnp.dot(curv, columns_k, preferred_element_type=F32)
        if k:
            parts[k] = lax.ppermute(part.astype(jnp.float16), "x", shift(4, k))
        else:
            share = part
    for k in (1, 3, 2):
        share = share + parts[k].astype(F32)

    share = share.reshape(8, rows // 4, quarter)
    packed = share.astype(jnp.float16)
    piece = take(share, z)
    for k in (4, 3, 5, 2, 6, 1, 7):
        piece = piece + lax.ppermute(take(packed, (z + k) % 8), Z, zshift(k)).astype(F32)

    packed = piece.astype(jnp.float16)
    line = jnp.zeros((4,) + packed.shape, jnp.float16)
    line = lax.dynamic_update_index_in_dim(line, packed, zl, 0)
    for k in (3, 1, 2):
        got = lax.ppermute(packed, "zl", shift(4, k))
        line = lax.dynamic_update_index_in_dim(line, got, (zl - k) % 4, 0)
    product = lax.all_gather(line.reshape(rows, quarter), "x", axis=0, tiled=False)
    coeff = beta_prev[0]
    me = (z * 4 + x) * 8 + lax.axis_index("y") * 2 + lax.axis_index("c")
    table = table_of(jnp.stack([me, zl, x]), jnp.stack([unit, coeff]), piece, cur, prev)
    table = sum_x(sum_z(sum_group(table)))
    entries = F32(16 * rows * depth)
    alpha = jnp.sum(table[0]) / entries
    gap = alpha - table[2]
    mean_sq = jnp.sum(table[3] - 2.0 * gap * table[4] + gap * gap * table[1]) / entries
    beta = jnp.sqrt(jnp.maximum(mean_sq, 0.0) + EPS_MEAN)
    product = product.transpose(1, 0, 2).reshape(rows, depth).astype(F32) * unit
    fresh = (product - alpha * cur - coeff * prev) / beta
    return (fresh, jnp.stack([alpha, beta]))


def solution(mesh):
    inner = Mesh(mesh.devices.reshape(4, 4, 4, 2, 2), ("zl", "x", "y", "zh", "c"))
    dp, shard = ("zl", "x"), ("y", "zh", "c")
    return jax.shard_map(
        per_device,
        mesh=inner,
        in_specs=(
            P(dp + shard, None),
            P(None, dp + shard),
            P(shard, None),
            P(shard, None),
            P(shard, None),
            P(),
        ),
        out_specs=(P(shard, None), P()),
        check_vma=False,
    )
```

```python
import jax
import jax.numpy as jnp
from jax import lax
from jax.experimental import pallas as pl
from jax.experimental.pallas import tpu as pltpu
from jax.sharding import Mesh, PartitionSpec as P

EPS_NORM = 1e-05
EPS_MEAN = 1e-06
PRODUCT_BOUND = 6.0 * 170.0
HALF_BITS = 15.0
Z = ("zl", "zh")
F32 = jnp.float32


def place(z):
    return (z % 4) * 2 + z // 4


def shift(n, k):
    return [(i, (i + k) % n) for i in range(n)]


def zshift(k):
    return [(place(i), place((i + k) % 8)) for i in range(8)]


def xor(n, k):
    return [(i, i ^ k) for i in range(n)]


def sum_group(v):
    v = v + lax.ppermute(v, "c", xor(2, 1))
    v = v + lax.ppermute(v, "y", xor(4, 1))
    return v + lax.ppermute(v, "y", xor(4, 3))


def from_x(v):
    return [lax.ppermute(v, "x", shift(4, k)) for k in (1, 3, 2)]


def from_z(v):
    return [lax.ppermute(v, Z, zshift(k)) for k in (4, 3, 5, 2, 6, 1, 7)]


def from_group(v):
    perms = [
        [(2 * y + c, 2 * ((y + k) % 4) + (c ^ j)) for y in range(4) for c in range(2)]
        for k in (2, 1, 3, 0)
        for j in (1, 0)
    ]
    return [lax.ppermute(v, ("y", "c"), perm) for perm in perms[:-1]]


def largest(v, others):
    for o in others:
        v = jnp.maximum(v, o)
    return v


def two_to(bits, bound):
    return jnp.clip(bits - jnp.ceil(jnp.log2(bound)), -100.0, 100.0)


def silu_terms(normed):
    sig = jax.nn.sigmoid(normed)
    first = sig * (1.0 + normed * (1.0 - sig))
    second = sig * (1.0 - sig) * (2.0 + normed * (1.0 - 2.0 * sig))
    return (sig, first, second)


def project_kernel(half, tok, w_own, w_other, d_own, d_other, hid, tan, sums, left):
    rows = w_own.shape[0]

    @pl.when(pl.program_id(0) == 0)
    def _():
        own = pl.multiple_of(half[0] * rows, 16)
        other = pl.multiple_of((1 - half[0]) * rows, 16)
        left[pl.ds(own, rows), :] = w_own[...]
        left[pl.ds(other, rows), :] = w_other[...]
        left[pl.ds(2 * rows + own, rows), :] = d_own[...]
        left[pl.ds(2 * rows + other, rows), :] = d_other[...]

    both = lax.dot_general(
        left[...], tok[...], (((1,), (1,)), ((), ())), preferred_element_type=F32
    )
    h, t = both[: 2 * rows], both[2 * rows :]
    hid[...] = h
    tan[...] = t
    sums[...] = jnp.zeros_like(sums)
    sums[0:1, :] = jnp.sum(h * h, 0, keepdims=True)
    sums[1:2, :] = jnp.sum(h * t, 0, keepdims=True)
    sums[2:3, :] = jnp.sum(t * t, 0, keepdims=True)


def project(half, gathered, w_own, w_other, d_own, d_other):
    rows, depth = w_own.shape
    count = gathered.shape[0]
    step = 256
    held = pl.BlockSpec((rows, depth), lambda i, h: (0, 0))
    out = pl.BlockSpec((2 * rows, step), lambda i, h: (0, i))
    return pl.pallas_call(
        project_kernel,
        out_shape=[
            jax.ShapeDtypeStruct((2 * rows, count), F32),
            jax.ShapeDtypeStruct((2 * rows, count), F32),
            jax.ShapeDtypeStruct((8, count), F32),
        ],
        grid_spec=pltpu.PrefetchScalarGridSpec(
            num_scalar_prefetch=1,
            grid=(count // step,),
            in_specs=[pl.BlockSpec((step, depth), lambda i, h: (i, 0)), held, held, held, held],
            out_specs=[out, out, pl.BlockSpec((8, step), lambda i, h: (0, i))],
            scratch_shapes=[pltpu.VMEM((4 * rows, depth), jnp.bfloat16)],
        ),
        compiler_params=pltpu.CompilerParams(vmem_limit_bytes=50 * 2**20),
        cost_estimate=pl.CostEstimate(
            flops=8 * rows * depth * count, bytes_accessed=2 * depth * (count + 4 * rows), transcendentals=0
        ),
    )(half, gathered, w_own, w_other, d_own, d_other)


def table_kernel(where, scalars, piece, cur, prev, out):
    unit, coeff = scalars[0], scalars[1]
    p, c = piece[...] * unit, cur[...]
    w = p - coeff * prev[...]
    dot_cc = jnp.sum(c * c)
    near = jnp.sum(w * c) / jnp.maximum(dot_cc, 1e-30)
    away = w - near * c
    rows = lax.broadcasted_iota(jnp.int32, out.shape, 0)
    values = (jnp.sum(c * p), dot_cc, near, jnp.sum(away * away), jnp.sum(away * c))
    table = jnp.zeros(out.shape, F32)
    for i, v in enumerate(values):
        table = jnp.where(rows == i, v, table)
    out[...] = jnp.where(lax.broadcasted_iota(jnp.int32, out.shape, 1) == where[0], table, 0.0)


def table_of(where, scalars, piece, cur, prev):
    at = pl.BlockSpec(piece.shape, lambda i, w: (w[1], w[2]))
    return pl.pallas_call(
        table_kernel,
        out_shape=jax.ShapeDtypeStruct((8, 256), F32),
        grid_spec=pltpu.PrefetchScalarGridSpec(
            num_scalar_prefetch=1,
            grid=(1,),
            in_specs=[
                pl.BlockSpec(memory_space=pltpu.SMEM),
                pl.BlockSpec(piece.shape, lambda i, w: (0, 0)),
                at,
                at,
            ],
            out_specs=pl.BlockSpec((8, 256), lambda i, w: (0, 0)),
        ),
    )(where, scalars, piece, cur, prev)


def curvature(hidden, tangent, sums, target, width, count):
    sums = sum_group(sums)
    squares, cross = sums[0], sums[1]
    scale = lax.rsqrt(squares / width + EPS_NORM)
    bound = jnp.sum(scale * scale * jnp.sqrt(sums[2])) * (PRODUCT_BOUND / count)
    bound = jnp.full((8, 128), bound, F32)
    bound = largest(bound, from_x(bound))
    power = two_to(HALF_BITS - 2.0, bound[0, 0])
    scale_dot = -(scale * scale * scale) * cross / width
    normed = hidden * scale
    normed_dot = tangent * scale + hidden * scale_dot
    sig, first, second = silu_terms(normed)
    error = normed * sig - target.astype(F32)
    grad_u = error * first / count
    grad_dot = (first * first + error * second) * normed_dot / count
    sums = sum_group(
        jnp.stack([jnp.sum(grad_u * hidden, 0), jnp.sum(grad_dot * hidden + grad_u * tangent, 0)])
    )
    inner = sums[0] / width
    inner_dot = sums[1] / width
    cube = scale * scale * scale
    result = (
        scale_dot * grad_u
        + scale * grad_dot
        - 3.0 * scale * scale * scale_dot * hidden * inner
        - cube * tangent * inner
        - cube * hidden * inner_dot
    )
    return (result * jnp.exp2(power)).astype(jnp.bfloat16), power, bound


def take(stack, index):
    return lax.dynamic_index_in_dim(stack, index, 0, keepdims=False)


def other_half(own, x):
    quarters = own.reshape(4, own.shape[0] // 4, own.shape[1])
    part = lax.ppermute(take(quarters, x), "zh", xor(2, 1))
    out = jnp.zeros_like(quarters)
    out = lax.dynamic_update_index_in_dim(out, part, x, 0)
    for k in (1, 3, 2):
        got = lax.ppermute(part, "x", shift(4, k))
        out = lax.dynamic_update_index_in_dim(out, got, (x - k) % 4, 0)
    return out.reshape(own.shape)


def per_device(tokens, targets, weight, cur, prev, beta_prev):
    x, zl, zh = (lax.axis_index(n) for n in ("x", "zl", "zh"))
    z = zh * 4 + zl
    width, own = targets.shape
    rows, depth = weight.shape
    total = own * 256

    gathered = lax.all_gather(tokens, ("y", "c"), axis=0, tiled=True)
    blocks = targets.reshape(4, 2, 2, rows, own).transpose(0, 2, 1, 3, 4).reshape(8, 2 * rows, own)
    columns = lax.all_to_all(blocks, ("y", "c"), split_axis=0, concat_axis=2, tiled=True)
    columns = columns.reshape(2 * rows, 8 * own)

    direction = cur.astype(jnp.bfloat16)
    hidden, tangent, sums = project(
        zh[None], gathered, weight, other_half(weight, x), direction, other_half(direction, x)
    )
    curv, power, bound = curvature(hidden, tangent, sums, columns, F32(width), F32(total))

    quarter = depth // 4
    parts = {}
    for k in (2, 1, 3, 0):
        columns_k = lax.dynamic_slice_in_dim(gathered, ((x + k) % 4) * quarter, quarter, 1)
        part = jnp.dot(curv, columns_k, preferred_element_type=F32)
        if k:
            parts[k] = lax.ppermute(part.astype(jnp.float16), "x", shift(4, k))
        else:
            share = part
    for k in (1, 3, 2):
        share = share + parts[k].astype(F32)

    shared = two_to(HALF_BITS - 5.0, largest(bound, from_z(bound))[0, 0])
    unit = jnp.exp2(-shared)
    share = share.reshape(8, rows // 4, quarter) * jnp.exp2(shared - power)
    packed = share.astype(jnp.float16)
    piece = take(share, z)
    for k in (4, 3, 5, 2, 6, 1, 7):
        piece = piece + lax.ppermute(take(packed, (z + k) % 8), Z, zshift(k)).astype(F32)

    coeff = beta_prev[0]
    me = (z * 4 + x) * 8 + lax.axis_index("y") * 2 + lax.axis_index("c")
    table = table_of(jnp.stack([me, zl, x]), jnp.stack([unit, coeff]), piece, cur, prev)
    packed = piece.astype(jnp.float16)
    line = jnp.zeros((4,) + packed.shape, jnp.float16)
    line = lax.dynamic_update_index_in_dim(line, packed, zl, 0)
    for k in (3, 1, 2):
        got = lax.ppermute(packed, "zl", shift(4, k))
        line = lax.dynamic_update_index_in_dim(line, got, (zl - k) % 4, 0)
    table = sum(from_group(table), table)
    line, table = lax.optimization_barrier((line.reshape(rows, quarter), table))
    blocks = [line] + [lax.ppermute(line, "x", shift(4, k)) for k in (1, 2, 3)]
    table = sum(from_z(table), table)
    *blocks, table = lax.optimization_barrier((*blocks, table))
    table = sum(from_x(table), table)
    entries = F32(16 * rows * depth)
    alpha = jnp.sum(table[0]) / entries
    gap = alpha - table[2]
    mean_sq = jnp.sum(table[3] - 2.0 * gap * table[4] + gap * gap * table[1]) / entries
    beta = jnp.sqrt(jnp.maximum(mean_sq, 0.0) + EPS_MEAN)
    fresh = jnp.zeros((rows, depth), F32)
    for k, block in enumerate(blocks):
        at = ((x - k) % 4) * quarter
        c = lax.dynamic_slice_in_dim(cur, at, quarter, 1)
        q = lax.dynamic_slice_in_dim(prev, at, quarter, 1)
        part = (block.astype(F32) * unit - alpha * c - coeff * q) / beta
        fresh = lax.dynamic_update_slice_in_dim(fresh, part, at, 1)
    return (fresh, jnp.stack([alpha, beta]))


def solution(mesh):
    inner = Mesh(mesh.devices.reshape(4, 4, 4, 2, 2), ("zl", "x", "y", "zh", "c"))
    dp, shard = ("zl", "x"), ("y", "zh", "c")
    return jax.shard_map(
        per_device,
        mesh=inner,
        in_specs=(
            P(dp + shard, None),
            P(None, dp + shard),
            P(shard, None),
            P(shard, None),
            P(shard, None),
            P(),
        ),
        out_specs=(P(shard, None), P()),
        check_vma=False,
    )
```

```python
import jax
import jax.numpy as jnp
from jax import lax
from jax.experimental import pallas as pl
from jax.experimental.pallas import tpu as pltpu
from jax.sharding import Mesh, PartitionSpec as P

EPS_NORM = 1e-05
EPS_MEAN = 1e-06
PRODUCT_BOUND = 6.0 * 170.0
HALF_BITS = 15.0
Z = ("zl", "zh")
F32 = jnp.float32


def place(z):
    return (z % 4) * 2 + z // 4


def shift(n, k):
    return [(i, (i + k) % n) for i in range(n)]


def zshift(k):
    return [(place(i), place((i + k) % 8)) for i in range(8)]


def xor(n, k):
    return [(i, i ^ k) for i in range(n)]


def sum_group(v):
    v = v + lax.ppermute(v, "c", xor(2, 1))
    v = v + lax.ppermute(v, "y", xor(4, 1))
    return v + lax.ppermute(v, "y", xor(4, 3))


def from_x(v):
    return [lax.ppermute(v, "x", shift(4, k)) for k in (1, 3, 2)]


def from_z(v):
    return [lax.ppermute(v, Z, zshift(k)) for k in (4, 3, 5, 2, 6, 1, 7)]


def from_group(v):
    perms = [
        [(2 * y + c, 2 * ((y + k) % 4) + (c ^ j)) for y in range(4) for c in range(2)]
        for k in (2, 1, 3, 0)
        for j in (1, 0)
    ]
    return [lax.ppermute(v, ("y", "c"), perm) for perm in perms[:-1]]


def largest(v, others):
    for o in others:
        v = jnp.maximum(v, o)
    return v


def two_to(bits, bound):
    return jnp.clip(bits - jnp.ceil(jnp.log2(bound)), -100.0, 100.0)


def silu_terms(normed):
    sig = jax.nn.sigmoid(normed)
    first = sig * (1.0 + normed * (1.0 - sig))
    second = sig * (1.0 - sig) * (2.0 + normed * (1.0 - 2.0 * sig))
    return (sig, first, second)


def project_kernel(half, tok, w_own, w_other, d_own, d_other, hid, tan, sums, left, sems):
    rows = w_own.shape[0]

    @pl.when(pl.program_id(0) == 0)
    def _():
        own = pl.multiple_of(half[0] * rows, 16)
        other = pl.multiple_of((1 - half[0]) * rows, 16)
        copies = [
            pltpu.make_async_copy(ref, left.at[pl.ds(at, rows), :], sems.at[i])
            for i, (ref, at) in enumerate(
                ((w_own, own), (w_other, other), (d_own, 2 * rows + own), (d_other, 2 * rows + other))
            )
        ]
        for copy in copies:
            copy.start()
        for copy in copies:
            copy.wait()

    both = lax.dot_general(
        left[...], tok[...], (((1,), (1,)), ((), ())), preferred_element_type=F32
    )
    h, t = both[: 2 * rows], both[2 * rows :]
    hid[...] = h
    tan[...] = t
    sums[...] = jnp.zeros_like(sums)
    sums[0:1, :] = jnp.sum(h * h, 0, keepdims=True)
    sums[1:2, :] = jnp.sum(h * t, 0, keepdims=True)
    sums[2:3, :] = jnp.sum(t * t, 0, keepdims=True)


def project(half, gathered, w_own, w_other, d_own, d_other):
    rows, depth = w_own.shape
    count = gathered.shape[0]
    step = 256
    held = pl.BlockSpec(memory_space=pl.ANY)
    out = pl.BlockSpec((2 * rows, step), lambda i, h: (0, i))
    return pl.pallas_call(
        project_kernel,
        out_shape=[
            jax.ShapeDtypeStruct((2 * rows, count), F32),
            jax.ShapeDtypeStruct((2 * rows, count), F32),
            jax.ShapeDtypeStruct((8, count), F32),
        ],
        grid_spec=pltpu.PrefetchScalarGridSpec(
            num_scalar_prefetch=1,
            grid=(count // step,),
            in_specs=[pl.BlockSpec((step, depth), lambda i, h: (i, 0)), held, held, held, held],
            out_specs=[out, out, pl.BlockSpec((8, step), lambda i, h: (0, i))],
            scratch_shapes=[
                pltpu.VMEM((4 * rows, depth), jnp.bfloat16),
                pltpu.SemaphoreType.DMA((4,)),
            ],
        ),
        compiler_params=pltpu.CompilerParams(vmem_limit_bytes=50 * 2**20),
        cost_estimate=pl.CostEstimate(
            flops=8 * rows * depth * count, bytes_accessed=2 * depth * (count + 4 * rows), transcendentals=0
        ),
    )(half, gathered, w_own, w_other, d_own, d_other)


def sums_kernel(scalars, product, cur, prev, out):
    unit, coeff = scalars[0], scalars[1]
    p, c = product[...] * unit, cur[...]
    w = p - coeff * prev[...]
    rows = lax.broadcasted_iota(jnp.int32, out.shape, 0)
    table = jnp.zeros(out.shape, F32)
    for i, v in enumerate((c * p, c * c, w * w, w * c)):
        table = jnp.where(rows == i, jnp.sum(v), table)

    @pl.when(pl.program_id(0) == 0)
    def _():
        out[...] = jnp.zeros_like(out)

    out[...] += table


def sums_of(scalars, product, cur, prev):
    rows, depth = cur.shape
    block = pl.BlockSpec((rows // 4, depth), lambda i: (i, 0))
    return pl.pallas_call(
        sums_kernel,
        out_shape=jax.ShapeDtypeStruct((8, 128), F32),
        grid=(4,),
        in_specs=[pl.BlockSpec(memory_space=pltpu.SMEM), block, block, block],
        out_specs=pl.BlockSpec((8, 128), lambda i: (0, 0)),
        compiler_params=pltpu.CompilerParams(vmem_limit_bytes=32 * 2**20),
    )(scalars, product, cur, prev)


def step_kernel(entries, scalars, table, product, cur, prev, fresh, coefficients):
    unit, coeff = scalars[0], scalars[1]
    t = table[...]
    dot_cp, dot_cc, dot_ww, dot_wc = (t[i : i + 1, 0:1] for i in range(4))
    alpha = dot_cp / entries
    mean_sq = (dot_ww - 2.0 * alpha * dot_wc + alpha * alpha * dot_cc) / entries
    beta = jnp.sqrt(jnp.maximum(mean_sq, 0.0) + EPS_MEAN)
    resid = product[...] * unit - alpha * cur[...] - coeff * prev[...]
    fresh[...] = resid * (1.0 / beta)
    lane = lax.broadcasted_iota(jnp.int32, coefficients.shape, 1)
    coefficients[...] = jnp.where(lane == 0, alpha, beta)


def step_of(entries, scalars, table, product, cur, prev):
    rows, depth = cur.shape
    block = pl.BlockSpec((rows // 4, depth), lambda i: (i, 0))
    small = pl.BlockSpec((8, 128), lambda i: (0, 0))
    return pl.pallas_call(
        lambda *refs: step_kernel(entries, *refs),
        out_shape=[jax.ShapeDtypeStruct((rows, depth), F32), jax.ShapeDtypeStruct((8, 128), F32)],
        grid=(4,),
        in_specs=[pl.BlockSpec(memory_space=pltpu.SMEM), small, block, block, block],
        out_specs=[block, small],
        compiler_params=pltpu.CompilerParams(vmem_limit_bytes=32 * 2**20),
    )(scalars, table, product, cur, prev)


def curvature(hidden, tangent, sums, target, width, count):
    sums = sum_group(sums)
    squares, cross = sums[0], sums[1]
    scale = lax.rsqrt(squares / width + EPS_NORM)
    bound = jnp.sum(scale * scale * jnp.sqrt(sums[2])) * (PRODUCT_BOUND / count)
    bound = jnp.full((8, 128), bound, F32)
    bound = largest(bound, from_x(bound))
    power = two_to(HALF_BITS - 2.0, bound[0, 0])
    scale_dot = -(scale * scale * scale) * cross / width
    normed = hidden * scale
    normed_dot = tangent * scale + hidden * scale_dot
    sig, first, second = silu_terms(normed)
    error = normed * sig - target.astype(F32)
    grad_u = error * first / count
    grad_dot = (first * first + error * second) * normed_dot / count
    sums = sum_group(
        jnp.stack([jnp.sum(grad_u * hidden, 0), jnp.sum(grad_dot * hidden + grad_u * tangent, 0)])
    )
    inner = sums[0] / width
    inner_dot = sums[1] / width
    cube = scale * scale * scale
    result = (
        scale_dot * grad_u
        + scale * grad_dot
        - 3.0 * scale * scale * scale_dot * hidden * inner
        - cube * tangent * inner
        - cube * hidden * inner_dot
    )
    return (result * jnp.exp2(power)).astype(jnp.bfloat16), power, bound


def take(stack, index):
    return lax.dynamic_index_in_dim(stack, index, 0, keepdims=False)


def other_half(own, x):
    quarters = own.reshape(4, own.shape[0] // 4, own.shape[1])
    part = lax.ppermute(take(quarters, x), "zh", xor(2, 1))
    out = jnp.zeros_like(quarters)
    out = lax.dynamic_update_index_in_dim(out, part, x, 0)
    for k in (1, 3, 2):
        got = lax.ppermute(part, "x", shift(4, k))
        out = lax.dynamic_update_index_in_dim(out, got, (x - k) % 4, 0)
    return out.reshape(own.shape)


def per_device(tokens, targets, weight, cur, prev, beta_prev):
    x, zl, zh = (lax.axis_index(n) for n in ("x", "zl", "zh"))
    z = zh * 4 + zl
    width, own = targets.shape
    rows, depth = weight.shape
    total = own * 256

    gathered = lax.all_gather(tokens, ("y", "c"), axis=0, tiled=True)
    blocks = targets.reshape(4, 2, 2, rows, own).transpose(0, 2, 1, 3, 4).reshape(8, 2 * rows, own)
    blocks, gathered = lax.optimization_barrier((blocks, gathered))
    columns = lax.all_to_all(blocks, ("y", "c"), split_axis=0, concat_axis=2, tiled=True)
    columns = columns.reshape(2 * rows, 8 * own)

    direction = cur.astype(jnp.bfloat16)
    hidden, tangent, sums = project(
        zh[None], gathered, weight, other_half(weight, x), direction, other_half(direction, x)
    )
    curv, power, bound = curvature(hidden, tangent, sums, columns, F32(width), F32(total))

    quarter = depth // 4
    parts = {}
    for k in (2, 1, 3, 0):
        columns_k = lax.dynamic_slice_in_dim(gathered, ((x + k) % 4) * quarter, quarter, 1)
        part = jnp.dot(curv, columns_k, preferred_element_type=F32)
        if k:
            parts[k] = lax.ppermute(part.astype(jnp.float16), "x", shift(4, k))
        else:
            share = part
    for k in (1, 3, 2):
        share = share + parts[k].astype(F32)

    shared = two_to(HALF_BITS - 5.0, largest(bound, from_z(bound))[0, 0])
    unit = jnp.exp2(-shared)
    share = share.reshape(8, rows // 4, quarter) * jnp.exp2(shared - power)
    packed = share.astype(jnp.float16)
    piece = take(share, z)
    for k in (4, 3, 5, 2, 6, 1, 7):
        piece = piece + lax.ppermute(take(packed, (z + k) % 8), Z, zshift(k)).astype(F32)

    packed = piece.astype(jnp.float16)
    line = jnp.zeros((4,) + packed.shape, jnp.float16)
    line = lax.dynamic_update_index_in_dim(line, packed, zl, 0)
    for k in (3, 1, 2):
        got = lax.ppermute(packed, "zl", shift(4, k))
        line = lax.dynamic_update_index_in_dim(line, got, (zl - k) % 4, 0)
    product = lax.all_gather(line.reshape(rows, quarter), "x", axis=0, tiled=False)
    product = product.transpose(1, 0, 2).reshape(rows, depth).astype(F32)

    scalars = jnp.stack([unit, beta_prev[0]])
    table = sum_group(sums_of(scalars, product, cur, prev))
    table = table + lax.ppermute(table, "zh", xor(2, 1))
    fresh, coefficients = step_of(float(16 * rows * depth), scalars, table, product, cur, prev)
    return (fresh, coefficients[0, :2])


def solution(mesh):
    inner = Mesh(mesh.devices.reshape(4, 4, 4, 2, 2), ("zl", "x", "y", "zh", "c"))
    dp, shard = ("zl", "x"), ("y", "zh", "c")
    return jax.shard_map(
        per_device,
        mesh=inner,
        in_specs=(
            P(dp + shard, None),
            P(None, dp + shard),
            P(shard, None),
            P(shard, None),
            P(shard, None),
            P(),
        ),
        out_specs=(P(shard, None), P()),
        check_vma=False,
    )
```

```python
import jax
import jax.numpy as jnp
from jax import lax
from jax.experimental import pallas as pl
from jax.experimental.pallas import tpu as pltpu
from jax.sharding import Mesh, PartitionSpec as P

EPS_NORM = 1e-05
EPS_MEAN = 1e-06
PRODUCT_BOUND = 6.0 * 170.0
HALF_BITS = 15.0
Z = ("zl", "zh")
F32 = jnp.float32


def place(z):
    return (z % 4) * 2 + z // 4


def shift(n, k):
    return [(i, (i + k) % n) for i in range(n)]


def zshift(k):
    return [(place(i), place((i + k) % 8)) for i in range(8)]


def xor(n, k):
    return [(i, i ^ k) for i in range(n)]


def sum_group(v):
    v = v + lax.ppermute(v, "c", xor(2, 1))
    v = v + lax.ppermute(v, "y", xor(4, 1))
    return v + lax.ppermute(v, "y", xor(4, 3))


def from_x(v):
    return [lax.ppermute(v, "x", shift(4, k)) for k in (1, 3, 2)]


def from_z(v):
    return [lax.ppermute(v, Z, zshift(k)) for k in (4, 3, 5, 2, 6, 1, 7)]


def from_group(v):
    perms = [
        [(2 * y + c, 2 * ((y + k) % 4) + (c ^ j)) for y in range(4) for c in range(2)]
        for k in (2, 1, 3, 0)
        for j in (1, 0)
    ]
    return [lax.ppermute(v, ("y", "c"), perm) for perm in perms[:-1]]


def largest(v, others):
    for o in others:
        v = jnp.maximum(v, o)
    return v


def two_to(bits, bound):
    return jnp.clip(bits - jnp.ceil(jnp.log2(bound)), -100.0, 100.0)


def silu_terms(normed):
    sig = jax.nn.sigmoid(normed)
    first = sig * (1.0 + normed * (1.0 - sig))
    second = sig * (1.0 - sig) * (2.0 + normed * (1.0 - 2.0 * sig))
    return (sig, first, second)


def project_kernel(place_of, *refs):
    tokens, mats = refs[:10], (refs[10:16], refs[16:22])
    hid, tan, sums, gathered = refs[22:26]
    left, tok, mat_sems, tok_sems, out_sems = refs[26:]
    i = pl.program_id(0)
    x, c, half = place_of[4], place_of[5], place_of[6]
    rows, depth = mats[0][0].shape
    own, quarter = tokens[0].shape[0], depth // 4
    own_at = pl.multiple_of(half * rows, 16)
    other_at = (1 - half) * rows

    def mat_copies():
        copies = []
        for m, parts in enumerate(mats):
            base = 2 * rows * m
            copies.append((parts[0], left.at[pl.ds(pl.multiple_of(base + own_at, 16), rows), :]))
            for part, back, row in zip(parts[1:], (0, 1, 3, 2, 2), (0, 0, 0, 0, rows // 2)):
                at = pl.multiple_of(lax.rem(x + 4 - back, 4) * quarter, 128)
                place = pl.multiple_of(base + other_at + row, 16)
                copies.append((part, left.at[pl.ds(place, part.shape[0]), pl.ds(at, quarter)]))
        return [pltpu.make_async_copy(f, t, mat_sems.at[n]) for n, (f, t) in enumerate(copies)]

    def tok_copies(chunk):
        mine, theirs = pl.multiple_of(c * own, 16), pl.multiple_of((1 - c) * own, 16)
        if chunk < 3:
            pairs = ((tokens[2 * chunk], mine), (tokens[2 * chunk + 1], theirs))
        else:
            pairs = ((tokens[6], mine), (tokens[7], mine + own // 2), (tokens[8], theirs), (tokens[9], theirs + own // 2))
        return [
            pltpu.make_async_copy(
                ref, tok.at[chunk, pl.ds(pl.multiple_of(at, 16), ref.shape[0]), :], tok_sems.at[2 * chunk + n]
            )
            for n, (ref, at) in enumerate(pairs)
        ]

    def out_copy(chunk):
        at = pl.multiple_of(place_of[chunk] * 2 * own, 16)
        return pltpu.make_async_copy(tok.at[chunk], gathered.at[pl.ds(at, 2 * own), :], out_sems.at[chunk])

    @pl.when(i == 0)
    def _():
        for copy in mat_copies():
            copy.start()
        for chunk in range(4):
            for copy in tok_copies(chunk):
                copy.start()
        for copy in mat_copies():
            copy.wait()

    for chunk in range(4):

        @pl.when(i == chunk)
        def _():
            for copy in tok_copies(chunk):
                copy.wait()
            out_copy(chunk).start()

    both = lax.dot_general(
        left[...], tok[i], (((1,), (1,)), ((), ())), preferred_element_type=F32
    )
    h, t = both[: 2 * rows], both[2 * rows :]
    hid[...] = h
    tan[...] = t
    sums[...] = jnp.zeros_like(sums)
    sums[0:1, :] = jnp.sum(h * h, 0, keepdims=True)
    sums[1:2, :] = jnp.sum(h * t, 0, keepdims=True)
    sums[2:3, :] = jnp.sum(t * t, 0, keepdims=True)

    @pl.when(i == 3)
    def _():
        for chunk in range(4):
            out_copy(chunk).wait()


def project(place_of, tokens, weight, direction):
    own, depth = tokens[0].shape
    rows = weight[0].shape[0]
    count, step = 8 * own, 2 * own
    held = pl.BlockSpec(memory_space=pl.ANY)
    out = pl.BlockSpec((2 * rows, step), lambda i, p: (0, p[i]))
    return pl.pallas_call(
        project_kernel,
        out_shape=[
            jax.ShapeDtypeStruct((2 * rows, count), F32),
            jax.ShapeDtypeStruct((2 * rows, count), F32),
            jax.ShapeDtypeStruct((8, count), F32),
            jax.ShapeDtypeStruct((count, depth), jnp.bfloat16),
        ],
        grid_spec=pltpu.PrefetchScalarGridSpec(
            num_scalar_prefetch=1,
            grid=(4,),
            in_specs=[held] * 22,
            out_specs=[out, out, pl.BlockSpec((8, step), lambda i, p: (0, p[i])), held],
            scratch_shapes=[
                pltpu.VMEM((4 * rows, depth), jnp.bfloat16),
                pltpu.VMEM((4, step, depth), jnp.bfloat16),
                pltpu.SemaphoreType.DMA((12,)),
                pltpu.SemaphoreType.DMA((10,)),
                pltpu.SemaphoreType.DMA((4,)),
            ],
        ),
        compiler_params=pltpu.CompilerParams(vmem_limit_bytes=50 * 2**20),
        cost_estimate=pl.CostEstimate(
            flops=8 * rows * depth * count, bytes_accessed=2 * depth * (2 * count + 4 * rows), transcendentals=0
        ),
    )(place_of, *tokens, *weight, *direction)


def sums_kernel(scalars, product, cur, prev, out):
    unit, coeff = scalars[0], scalars[1]
    p, c = product[...] * unit, cur[...]
    w = p - coeff * prev[...]
    rows = lax.broadcasted_iota(jnp.int32, out.shape, 0)
    table = jnp.zeros(out.shape, F32)
    for i, v in enumerate((c * p, c * c, w * w, w * c)):
        table = jnp.where(rows == i, jnp.sum(v), table)

    @pl.when(pl.program_id(0) == 0)
    def _():
        out[...] = jnp.zeros_like(out)

    out[...] += table


def sums_of(scalars, product, cur, prev):
    rows, depth = cur.shape
    block = pl.BlockSpec((rows // 4, depth), lambda i: (i, 0))
    return pl.pallas_call(
        sums_kernel,
        out_shape=jax.ShapeDtypeStruct((8, 128), F32),
        grid=(4,),
        in_specs=[pl.BlockSpec(memory_space=pltpu.SMEM), block, block, block],
        out_specs=pl.BlockSpec((8, 128), lambda i: (0, 0)),
        compiler_params=pltpu.CompilerParams(vmem_limit_bytes=32 * 2**20),
    )(scalars, product, cur, prev)


def step_kernel(entries, scalars, table, product, cur, prev, fresh, coefficients):
    unit, coeff = scalars[0], scalars[1]
    t = table[...]
    dot_cp, dot_cc, dot_ww, dot_wc = (t[i : i + 1, 0:1] for i in range(4))
    alpha = dot_cp / entries
    mean_sq = (dot_ww - 2.0 * alpha * dot_wc + alpha * alpha * dot_cc) / entries
    beta = jnp.sqrt(jnp.maximum(mean_sq, 0.0) + EPS_MEAN)
    resid = product[...] * unit - alpha * cur[...] - coeff * prev[...]
    fresh[...] = resid * (1.0 / beta)
    lane = lax.broadcasted_iota(jnp.int32, coefficients.shape, 1)
    coefficients[...] = jnp.where(lane == 0, alpha, beta)


def step_of(entries, scalars, table, product, cur, prev):
    rows, depth = cur.shape
    block = pl.BlockSpec((rows // 4, depth), lambda i: (i, 0))
    small = pl.BlockSpec((8, 128), lambda i: (0, 0))
    return pl.pallas_call(
        lambda *refs: step_kernel(entries, *refs),
        out_shape=[jax.ShapeDtypeStruct((rows, depth), F32), jax.ShapeDtypeStruct((8, 128), F32)],
        grid=(4,),
        in_specs=[pl.BlockSpec(memory_space=pltpu.SMEM), small, block, block, block],
        out_specs=[block, small],
        compiler_params=pltpu.CompilerParams(vmem_limit_bytes=32 * 2**20),
    )(scalars, table, product, cur, prev)


def curvature(hidden, tangent, sums, target, width, count):
    sums = sum_group(sums)
    squares, cross = sums[0], sums[1]
    scale = lax.rsqrt(squares / width + EPS_NORM)
    bound = jnp.sum(scale * scale * jnp.sqrt(sums[2])) * (PRODUCT_BOUND / count)
    bound = jnp.full((8, 128), bound, F32)
    bound = largest(bound, from_x(bound))
    power = two_to(HALF_BITS - 2.0, bound[0, 0])
    scale_dot = -(scale * scale * scale) * cross / width
    normed = hidden * scale
    normed_dot = tangent * scale + hidden * scale_dot
    sig, first, second = silu_terms(normed)
    error = normed * sig - target.astype(F32)
    grad_u = error * first / count
    grad_dot = (first * first + error * second) * normed_dot / count
    sums = sum_group(
        jnp.stack([jnp.sum(grad_u * hidden, 0), jnp.sum(grad_dot * hidden + grad_u * tangent, 0)])
    )
    inner = sums[0] / width
    inner_dot = sums[1] / width
    cube = scale * scale * scale
    result = (
        scale_dot * grad_u
        + scale * grad_dot
        - 3.0 * scale * scale * scale_dot * hidden * inner
        - cube * tangent * inner
        - cube * hidden * inner_dot
    )
    return (result * jnp.exp2(power)).astype(jnp.bfloat16), power, bound


def take(stack, index):
    return lax.dynamic_index_in_dim(stack, index, 0, keepdims=False)


def ring(own, axis):
    half = own.shape[0] // 2
    back = lax.ppermute(own, axis, shift(4, 1))
    ahead = lax.ppermute(own, axis, shift(4, 3))
    far = lax.ppermute(back[:half], axis, shift(4, 1)), lax.ppermute(ahead[half:], axis, shift(4, 3))
    return back, ahead, *far


def other_half(own, x):
    quarter = own.shape[1] // 4
    part = lax.ppermute(lax.dynamic_slice_in_dim(own, x * quarter, quarter, 1), "zh", xor(2, 1))
    return own, part, *ring(part, "x")


def token_group(own):
    back, ahead, *far = ring(own, "y")
    swap = lambda v: lax.ppermute(v, "c", xor(2, 1))
    pairs = [v for block in (own, back, ahead) for v in (block, swap(block))]
    return (*pairs, *far, *[swap(v) for v in far])


def per_device(tokens, targets, weight, cur, prev, beta_prev):
    x, zl, zh = (lax.axis_index(n) for n in ("x", "zl", "zh"))
    z = zh * 4 + zl
    width, own = targets.shape
    rows, depth = weight.shape
    total = own * 256

    y, core = lax.axis_index("y"), lax.axis_index("c")
    group = token_group(tokens)
    blocks = targets.reshape(4, 2, 2, rows, own).transpose(0, 2, 1, 3, 4).reshape(8, 2 * rows, own)
    blocks, last = lax.optimization_barrier((blocks, group[-1]))
    group = (*group[:-1], last)
    columns = lax.all_to_all(blocks, ("y", "c"), split_axis=0, concat_axis=2, tiled=True)
    columns = columns.reshape(2 * rows, 8 * own)

    place_of = jnp.stack([y, (y + 3) % 4, (y + 1) % 4, (y + 2) % 4, x, core, zh])
    hidden, tangent, sums, gathered = project(
        place_of, group, other_half(weight, x), other_half(cur.astype(jnp.bfloat16), x)
    )
    curv, power, bound = curvature(hidden, tangent, sums, columns, F32(width), F32(total))

    quarter = depth // 4
    parts = {}
    for k in (2, 1, 3, 0):
        columns_k = lax.dynamic_slice_in_dim(gathered, ((x + k) % 4) * quarter, quarter, 1)
        part = jnp.dot(curv, columns_k, preferred_element_type=F32)
        if k:
            parts[k] = lax.ppermute(part.astype(jnp.float16), "x", shift(4, k))
        else:
            share = part
    for k in (1, 3, 2):
        share = share + parts[k].astype(F32)

    shared = two_to(HALF_BITS - 5.0, largest(bound, from_z(bound))[0, 0])
    unit = jnp.exp2(-shared)
    share = share.reshape(8, rows // 4, quarter) * jnp.exp2(shared - power)
    packed = share.astype(jnp.float16)
    piece = take(share, z)
    for k in (4, 3, 5, 2, 6, 1, 7):
        piece = piece + lax.ppermute(take(packed, (z + k) % 8), Z, zshift(k)).astype(F32)

    packed = piece.astype(jnp.float16)
    line = jnp.zeros((4,) + packed.shape, jnp.float16)
    line = lax.dynamic_update_index_in_dim(line, packed, zl, 0)
    for k in (3, 1, 2):
        got = lax.ppermute(packed, "zl", shift(4, k))
        line = lax.dynamic_update_index_in_dim(line, got, (zl - k) % 4, 0)
    product = lax.all_gather(line.reshape(rows, quarter), "x", axis=0, tiled=False)
    product = product.transpose(1, 0, 2).reshape(rows, depth).astype(F32)

    scalars = jnp.stack([unit, beta_prev[0]])
    table = sum_group(sums_of(scalars, product, cur, prev))
    table = table + lax.ppermute(table, "zh", xor(2, 1))
    fresh, coefficients = step_of(float(16 * rows * depth), scalars, table, product, cur, prev)
    return (fresh, coefficients[0, :2])


def solution(mesh):
    inner = Mesh(mesh.devices.reshape(4, 4, 4, 2, 2), ("zl", "x", "y", "zh", "c"))
    dp, shard = ("zl", "x"), ("y", "zh", "c")
    return jax.shard_map(
        per_device,
        mesh=inner,
        in_specs=(
            P(dp + shard, None),
            P(None, dp + shard),
            P(shard, None),
            P(shard, None),
            P(shard, None),
            P(),
        ),
        out_specs=(P(shard, None), P()),
        check_vma=False,
    )
```

```python
import jax
import jax.numpy as jnp
from jax import lax
from jax.experimental import pallas as pl
from jax.experimental.pallas import tpu as pltpu
from jax.sharding import Mesh, PartitionSpec as P

EPS_NORM = 1e-05
EPS_MEAN = 1e-06
PRODUCT_BOUND = 6.0 * 170.0
HALF_BITS = 15.0
Z = ("zl", "zh")
F32 = jnp.float32


def place(z):
    return (z % 4) * 2 + z // 4


def shift(n, k):
    return [(i, (i + k) % n) for i in range(n)]


def zshift(k):
    return [(place(i), place((i + k) % 8)) for i in range(8)]


def xor(n, k):
    return [(i, i ^ k) for i in range(n)]


def sum_group(v):
    v = v + lax.ppermute(v, "c", xor(2, 1))
    v = v + lax.ppermute(v, "y", xor(4, 1))
    return v + lax.ppermute(v, "y", xor(4, 3))


def from_x(v):
    return [lax.ppermute(v, "x", shift(4, k)) for k in (1, 3, 2)]


def from_z(v):
    return [lax.ppermute(v, Z, zshift(k)) for k in (4, 3, 5, 2, 6, 1, 7)]


def from_group(v):
    perms = [
        [(2 * y + c, 2 * ((y + k) % 4) + (c ^ j)) for y in range(4) for c in range(2)]
        for k in (2, 1, 3, 0)
        for j in (1, 0)
    ]
    return [lax.ppermute(v, ("y", "c"), perm) for perm in perms[:-1]]


def largest(v, others):
    for o in others:
        v = jnp.maximum(v, o)
    return v


def two_to(bits, bound):
    return jnp.clip(bits - jnp.ceil(jnp.log2(bound)), -100.0, 100.0)


def silu_terms(normed):
    sig = jax.nn.sigmoid(normed)
    first = sig * (1.0 + normed * (1.0 - sig))
    second = sig * (1.0 - sig) * (2.0 + normed * (1.0 - 2.0 * sig))
    return (sig, first, second)


def project_kernel(place_of, *refs):
    tokens, mats = refs[:10], (refs[10:16], refs[16:22])
    hid, tan, sums, gathered = refs[22:26]
    left, tok, mat_sems, tok_sems, out_sems = refs[26:]
    i = pl.program_id(0)
    x, c, half = place_of[4], place_of[5], place_of[6]
    rows, depth = mats[0][0].shape
    own, quarter = tokens[0].shape[0], depth // 4
    own_at = pl.multiple_of(half * rows, 16)
    other_at = (1 - half) * rows

    def mat_copies():
        copies = []
        for m, parts in enumerate(mats):
            base = 2 * rows * m
            copies.append((parts[0], left.at[pl.ds(pl.multiple_of(base + own_at, 16), rows), :]))
            for part, back, row in zip(parts[1:], (0, 1, 3, 2, 2), (0, 0, 0, 0, rows // 2)):
                at = pl.multiple_of(lax.rem(x + 4 - back, 4) * quarter, 128)
                place = pl.multiple_of(base + other_at + row, 16)
                copies.append((part, left.at[pl.ds(place, part.shape[0]), pl.ds(at, quarter)]))
        return [pltpu.make_async_copy(f, t, mat_sems.at[n]) for n, (f, t) in enumerate(copies)]

    def tok_copies(chunk):
        mine, theirs = pl.multiple_of(c * own, 16), pl.multiple_of((1 - c) * own, 16)
        if chunk < 3:
            pairs = ((tokens[2 * chunk], mine), (tokens[2 * chunk + 1], theirs))
        else:
            pairs = ((tokens[6], mine), (tokens[7], mine + own // 2), (tokens[8], theirs), (tokens[9], theirs + own // 2))
        return [
            pltpu.make_async_copy(
                ref, tok.at[chunk, pl.ds(pl.multiple_of(at, 16), ref.shape[0]), :], tok_sems.at[2 * chunk + n]
            )
            for n, (ref, at) in enumerate(pairs)
        ]

    def out_copy(chunk):
        at = pl.multiple_of(place_of[chunk] * 2 * own, 16)
        return pltpu.make_async_copy(tok.at[chunk], gathered.at[pl.ds(at, 2 * own), :], out_sems.at[chunk])

    @pl.when(i == 0)
    def _():
        for copy in mat_copies():
            copy.start()
        for chunk in range(4):
            for copy in tok_copies(chunk):
                copy.start()
        for copy in mat_copies():
            copy.wait()

    for chunk in range(4):

        @pl.when(i == chunk)
        def _():
            for copy in tok_copies(chunk):
                copy.wait()
            out_copy(chunk).start()

    both = lax.dot_general(
        left[...], tok[i], (((1,), (1,)), ((), ())), preferred_element_type=F32
    )
    h, t = both[: 2 * rows], both[2 * rows :]
    hid[...] = h
    tan[...] = t
    sums[...] = jnp.zeros_like(sums)
    sums[0:1, :] = jnp.sum(h * h, 0, keepdims=True)
    sums[1:2, :] = jnp.sum(h * t, 0, keepdims=True)
    sums[2:3, :] = jnp.sum(t * t, 0, keepdims=True)

    @pl.when(i == 3)
    def _():
        for chunk in range(4):
            out_copy(chunk).wait()


def project(place_of, tokens, weight, direction):
    own, depth = tokens[0].shape
    rows = weight[0].shape[0]
    count, step = 8 * own, 2 * own
    held = pl.BlockSpec(memory_space=pl.ANY)
    out = pl.BlockSpec((2 * rows, step), lambda i, p: (0, p[i]))
    return pl.pallas_call(
        project_kernel,
        out_shape=[
            jax.ShapeDtypeStruct((2 * rows, count), F32),
            jax.ShapeDtypeStruct((2 * rows, count), F32),
            jax.ShapeDtypeStruct((8, count), F32),
            jax.ShapeDtypeStruct((count, depth), jnp.bfloat16),
        ],
        grid_spec=pltpu.PrefetchScalarGridSpec(
            num_scalar_prefetch=1,
            grid=(4,),
            in_specs=[held] * 22,
            out_specs=[out, out, pl.BlockSpec((8, step), lambda i, p: (0, p[i])), held],
            scratch_shapes=[
                pltpu.VMEM((4 * rows, depth), jnp.bfloat16),
                pltpu.VMEM((4, step, depth), jnp.bfloat16),
                pltpu.SemaphoreType.DMA((12,)),
                pltpu.SemaphoreType.DMA((10,)),
                pltpu.SemaphoreType.DMA((4,)),
            ],
        ),
        compiler_params=pltpu.CompilerParams(vmem_limit_bytes=50 * 2**20),
        cost_estimate=pl.CostEstimate(
            flops=8 * rows * depth * count, bytes_accessed=2 * depth * (2 * count + 4 * rows), transcendentals=0
        ),
    )(place_of, *tokens, *weight, *direction)


def sums_kernel(scalars, product, cur, prev, out):
    unit, coeff = scalars[0], scalars[1]
    p, c = product[...] * unit, cur[...]
    w = p - coeff * prev[...]
    rows = lax.broadcasted_iota(jnp.int32, out.shape, 0)
    table = jnp.zeros(out.shape, F32)
    for i, v in enumerate((c * p, c * c, w * w, w * c)):
        table = jnp.where(rows == i, jnp.sum(v), table)

    @pl.when(pl.program_id(0) == 0)
    def _():
        out[...] = jnp.zeros_like(out)

    out[...] += table


def sums_of(scalars, product, cur, prev):
    rows, depth = cur.shape
    block = pl.BlockSpec((rows // 4, depth), lambda i: (i, 0))
    return pl.pallas_call(
        sums_kernel,
        out_shape=jax.ShapeDtypeStruct((8, 128), F32),
        grid=(4,),
        in_specs=[pl.BlockSpec(memory_space=pltpu.SMEM), block, block, block],
        out_specs=pl.BlockSpec((8, 128), lambda i: (0, 0)),
        compiler_params=pltpu.CompilerParams(vmem_limit_bytes=32 * 2**20),
    )(scalars, product, cur, prev)


def step_kernel(entries, scalars, table, product, cur, prev, fresh, coefficients):
    unit, coeff = scalars[0], scalars[1]
    t = table[...]
    dot_cp, dot_cc, dot_ww, dot_wc = (t[i : i + 1, 0:1] for i in range(4))
    alpha = dot_cp / entries
    mean_sq = (dot_ww - 2.0 * alpha * dot_wc + alpha * alpha * dot_cc) / entries
    beta = jnp.sqrt(jnp.maximum(mean_sq, 0.0) + EPS_MEAN)
    resid = product[...] * unit - alpha * cur[...] - coeff * prev[...]
    fresh[...] = resid * (1.0 / beta)
    lane = lax.broadcasted_iota(jnp.int32, coefficients.shape, 1)
    coefficients[...] = jnp.where(lane == 0, alpha, beta)


def step_of(entries, scalars, table, product, cur, prev):
    rows, depth = cur.shape
    block = pl.BlockSpec((rows // 4, depth), lambda i: (i, 0))
    small = pl.BlockSpec((8, 128), lambda i: (0, 0))
    return pl.pallas_call(
        lambda *refs: step_kernel(entries, *refs),
        out_shape=[jax.ShapeDtypeStruct((rows, depth), F32), jax.ShapeDtypeStruct((8, 128), F32)],
        grid=(4,),
        in_specs=[pl.BlockSpec(memory_space=pltpu.SMEM), small, block, block, block],
        out_specs=[block, small],
        compiler_params=pltpu.CompilerParams(vmem_limit_bytes=32 * 2**20),
    )(scalars, table, product, cur, prev)


def curvature(hidden, tangent, sums, target, width, count):
    sums = sum_group(sums)
    squares, cross = sums[0], sums[1]
    scale = lax.rsqrt(squares / width + EPS_NORM)
    bound = jnp.sum(scale * scale * jnp.sqrt(sums[2])) * (PRODUCT_BOUND / count)
    bound = jnp.full((8, 128), bound, F32)
    bound = largest(bound, from_x(bound))
    power = two_to(HALF_BITS - 2.0, bound[0, 0])
    scale_dot = -(scale * scale * scale) * cross / width
    normed = hidden * scale
    normed_dot = tangent * scale + hidden * scale_dot
    sig, first, second = silu_terms(normed)
    error = normed * sig - target.astype(F32)
    grad_u = error * first / count
    grad_dot = (first * first + error * second) * normed_dot / count
    sums = sum_group(
        jnp.stack([jnp.sum(grad_u * hidden, 0), jnp.sum(grad_dot * hidden + grad_u * tangent, 0)])
    )
    inner = sums[0] / width
    inner_dot = sums[1] / width
    cube = scale * scale * scale
    result = (
        scale_dot * grad_u
        + scale * grad_dot
        - 3.0 * scale * scale * scale_dot * hidden * inner
        - cube * tangent * inner
        - cube * hidden * inner_dot
    )
    return (result * jnp.exp2(power)).astype(jnp.bfloat16), power, bound


def take(stack, index):
    return lax.dynamic_index_in_dim(stack, index, 0, keepdims=False)


def ring(own, axis):
    half = own.shape[0] // 2
    back = lax.ppermute(own, axis, shift(4, 1))
    ahead = lax.ppermute(own, axis, shift(4, 3))
    far = lax.ppermute(back[:half], axis, shift(4, 1)), lax.ppermute(ahead[half:], axis, shift(4, 3))
    return back, ahead, *far


def direct(own, axis):
    half = own.shape[0] // 2
    far = lax.ppermute(own, axis, shift(4, 2))
    return lax.ppermute(own, axis, shift(4, 1)), lax.ppermute(own, axis, shift(4, 3)), far[:half], far[half:]


def over_z(own, x):
    quarter = own.shape[1] // 4
    return lax.ppermute(lax.dynamic_slice_in_dim(own, x * quarter, quarter, 1), "zh", xor(2, 1))


def swap_core(v):
    return lax.ppermute(v, "c", xor(2, 1))


def per_device(tokens, targets, weight, cur, prev, beta_prev):
    x, zl, zh = (lax.axis_index(n) for n in ("x", "zl", "zh"))
    z = zh * 4 + zl
    width, own = targets.shape
    rows, depth = weight.shape
    total = own * 256

    y, core = lax.axis_index("y"), lax.axis_index("c")
    direction = cur.astype(jnp.bfloat16)
    weight_part, direction_part = over_z(weight, x), over_z(direction, x)
    half = own // 2
    back, ahead = lax.ppermute(tokens, "y", shift(4, 1)), lax.ppermute(tokens, "y", shift(4, 3))
    direction_part, *far = lax.optimization_barrier((direction_part, back[:half], ahead[half:]))
    far = [lax.ppermute(far[0], "y", shift(4, 1)), lax.ppermute(far[1], "y", shift(4, 3))]
    pairs = [v for block in (tokens, back, ahead) for v in (block, swap_core(block))]
    group = (*pairs, *far, *[swap_core(v) for v in far])
    blocks = targets.reshape(4, 2, 2, rows, own).transpose(0, 2, 1, 3, 4).reshape(8, 2 * rows, own)
    blocks, last = lax.optimization_barrier((blocks, group[-1]))
    group = (*group[:-1], last)
    columns = lax.all_to_all(blocks, ("y", "c"), split_axis=0, concat_axis=2, tiled=True)
    columns = columns.reshape(2 * rows, 8 * own)

    place_of = jnp.stack([y, (y + 3) % 4, (y + 1) % 4, (y + 2) % 4, x, core, zh])
    hidden, tangent, sums, gathered = project(
        place_of,
        group,
        (weight, weight_part, *ring(weight_part, "x")),
        (direction, direction_part, *direct(direction_part, "x")),
    )
    curv, power, bound = curvature(hidden, tangent, sums, columns, F32(width), F32(total))

    quarter, f16 = depth // 4, jnp.float16

    def partial(k):
        block = lax.dynamic_slice_in_dim(gathered, ((x + k) % 4) * quarter, quarter, 1)
        return jnp.dot(curv, block, preferred_element_type=F32)

    far = partial(2).astype(f16)
    up = lax.ppermute(far[:rows], "x", shift(4, 1))
    down = lax.ppermute(far[rows:], "x", shift(4, 3))
    near_up, near_down = partial(1), partial(3)
    near_up = jnp.concatenate([near_up[:rows] + up.astype(F32), near_up[rows:]])
    near_down = jnp.concatenate([near_down[:rows], near_down[rows:] + down.astype(F32)])
    up = lax.ppermute(near_up.astype(f16), "x", shift(4, 1))
    down = lax.ppermute(near_down.astype(f16), "x", shift(4, 3))
    share = partial(0) + up.astype(F32) + down.astype(F32)

    shared = two_to(HALF_BITS - 5.0, largest(bound, from_z(bound))[0, 0])
    unit = jnp.exp2(-shared)
    share = share.reshape(8, rows // 4, quarter) * jnp.exp2(shared - power)
    packed = share.astype(jnp.float16)
    piece = take(share, z)
    for k in (4, 3, 5, 2, 6, 1, 7):
        piece = piece + lax.ppermute(take(packed, (z + k) % 8), Z, zshift(k)).astype(F32)

    packed = piece.astype(jnp.float16)
    line = jnp.zeros((4,) + packed.shape, jnp.float16)
    line = lax.dynamic_update_index_in_dim(line, packed, zl, 0)
    for k in (3, 1, 2):
        got = lax.ppermute(packed, "zl", shift(4, k))
        line = lax.dynamic_update_index_in_dim(line, got, (zl - k) % 4, 0)
    product = lax.all_gather(line.reshape(rows, quarter), "x", axis=0, tiled=False)
    product = product.transpose(1, 0, 2).reshape(rows, depth).astype(F32)

    scalars = jnp.stack([unit, beta_prev[0]])
    table = sum_group(sums_of(scalars, product, cur, prev))
    table = table + lax.ppermute(table, "zh", xor(2, 1))
    fresh, coefficients = step_of(float(16 * rows * depth), scalars, table, product, cur, prev)
    return (fresh, coefficients[0, :2])


def solution(mesh):
    inner = Mesh(mesh.devices.reshape(4, 4, 4, 2, 2), ("zl", "x", "y", "zh", "c"))
    dp, shard = ("zl", "x"), ("y", "zh", "c")
    return jax.shard_map(
        per_device,
        mesh=inner,
        in_specs=(
            P(dp + shard, None),
            P(None, dp + shard),
            P(shard, None),
            P(shard, None),
            P(shard, None),
            P(),
        ),
        out_specs=(P(shard, None), P()),
        check_vma=False,
    )
```

```python
import jax
import jax.numpy as jnp
from jax import lax
from jax.experimental import pallas as pl
from jax.experimental.pallas import tpu as pltpu
from jax.sharding import Mesh, PartitionSpec as P

EPS_NORM = 1e-05
EPS_MEAN = 1e-06
PRODUCT_BOUND = 6.0 * 170.0
HALF_BITS = 15.0
Z = ("zl", "zh")
F32 = jnp.float32


def place(z):
    return (z % 4) * 2 + z // 4


def shift(n, k):
    return [(i, (i + k) % n) for i in range(n)]


def zshift(k):
    return [(place(i), place((i + k) % 8)) for i in range(8)]


def xor(n, k):
    return [(i, i ^ k) for i in range(n)]


def sum_group(v):
    v = v + lax.ppermute(v, "c", xor(2, 1))
    v = v + lax.ppermute(v, "y", xor(4, 1))
    return v + lax.ppermute(v, "y", xor(4, 3))


def max_x(v):
    for k in (1, 3):
        v = jnp.maximum(v, lax.ppermute(v, "x", xor(4, k)))
    return v


def max_z(v):
    for k in (1, 2, 4):
        v = jnp.maximum(v, lax.ppermute(v, Z, [(place(i), place(i ^ k)) for i in range(8)]))
    return v


def two_to(bits, bound):
    return jnp.clip(bits - jnp.ceil(jnp.log2(bound)), -100.0, 100.0)


def silu_terms(normed):
    sig = jax.nn.sigmoid(normed)
    first = sig * (1.0 + normed * (1.0 - sig))
    second = sig * (1.0 - sig) * (2.0 + normed * (1.0 - 2.0 * sig))
    return (sig, first, second)


def project_kernel(place_of, *refs):
    tokens, mats = refs[:10], (refs[10:16], refs[16:22])
    hid, tan, sums, gathered = refs[22:26]
    left, tok, mat_sems, tok_sems, out_sems = refs[26:]
    i = pl.program_id(0)
    x, c, half = place_of[4], place_of[5], place_of[6]
    rows, depth = mats[0][0].shape
    own, quarter = tokens[0].shape[0], depth // 4
    own_at = pl.multiple_of(half * rows, 16)
    other_at = (1 - half) * rows

    def mat_copies():
        copies = []
        for m, parts in enumerate(mats):
            base = 2 * rows * m
            copies.append((parts[0], left.at[pl.ds(pl.multiple_of(base + own_at, 16), rows), :]))
            for part, back, row in zip(parts[1:], (0, 1, 3, 2, 2), (0, 0, 0, 0, rows // 2)):
                at = pl.multiple_of(lax.rem(x + 4 - back, 4) * quarter, 128)
                place = pl.multiple_of(base + other_at + row, 16)
                copies.append((part, left.at[pl.ds(place, part.shape[0]), pl.ds(at, quarter)]))
        return [pltpu.make_async_copy(f, t, mat_sems.at[n]) for n, (f, t) in enumerate(copies)]

    def tok_copies(chunk):
        mine, theirs = pl.multiple_of(c * own, 16), pl.multiple_of((1 - c) * own, 16)
        if chunk < 3:
            pairs = ((tokens[2 * chunk], mine), (tokens[2 * chunk + 1], theirs))
        else:
            pairs = ((tokens[6], mine), (tokens[7], mine + own // 2), (tokens[8], theirs), (tokens[9], theirs + own // 2))
        return [
            pltpu.make_async_copy(
                ref, tok.at[chunk, pl.ds(pl.multiple_of(at, 16), ref.shape[0]), :], tok_sems.at[2 * chunk + n]
            )
            for n, (ref, at) in enumerate(pairs)
        ]

    def out_copy(chunk):
        at = pl.multiple_of(place_of[chunk] * 2 * own, 16)
        return pltpu.make_async_copy(tok.at[chunk], gathered.at[pl.ds(at, 2 * own), :], out_sems.at[chunk])

    @pl.when(i == 0)
    def _():
        for copy in mat_copies():
            copy.start()
        for chunk in range(4):
            for copy in tok_copies(chunk):
                copy.start()
        for copy in mat_copies():
            copy.wait()

    for chunk in range(4):

        @pl.when(i == chunk)
        def _():
            for copy in tok_copies(chunk):
                copy.wait()
            out_copy(chunk).start()

    both = lax.dot_general(
        left[...], tok[i], (((1,), (1,)), ((), ())), preferred_element_type=F32
    )
    h, t = both[: 2 * rows], both[2 * rows :]
    hid[...] = h
    tan[...] = t
    sums[...] = jnp.zeros_like(sums)
    sums[0:1, :] = jnp.sum(h * h, 0, keepdims=True)
    sums[1:2, :] = jnp.sum(h * t, 0, keepdims=True)
    sums[2:3, :] = jnp.sum(t * t, 0, keepdims=True)

    @pl.when(i == 3)
    def _():
        for chunk in range(4):
            out_copy(chunk).wait()


def project(place_of, tokens, weight, direction):
    own, depth = tokens[0].shape
    rows = weight[0].shape[0]
    count, step = 8 * own, 2 * own
    held = pl.BlockSpec(memory_space=pl.ANY)
    out = pl.BlockSpec((2 * rows, step), lambda i, p: (0, p[i]))
    return pl.pallas_call(
        project_kernel,
        out_shape=[
            jax.ShapeDtypeStruct((2 * rows, count), F32),
            jax.ShapeDtypeStruct((2 * rows, count), F32),
            jax.ShapeDtypeStruct((8, count), F32),
            jax.ShapeDtypeStruct((count, depth), jnp.bfloat16),
        ],
        grid_spec=pltpu.PrefetchScalarGridSpec(
            num_scalar_prefetch=1,
            grid=(4,),
            in_specs=[held] * 22,
            out_specs=[out, out, pl.BlockSpec((8, step), lambda i, p: (0, p[i])), held],
            scratch_shapes=[
                pltpu.VMEM((4 * rows, depth), jnp.bfloat16),
                pltpu.VMEM((4, step, depth), jnp.bfloat16),
                pltpu.SemaphoreType.DMA((12,)),
                pltpu.SemaphoreType.DMA((10,)),
                pltpu.SemaphoreType.DMA((4,)),
            ],
        ),
        compiler_params=pltpu.CompilerParams(vmem_limit_bytes=50 * 2**20),
        cost_estimate=pl.CostEstimate(
            flops=8 * rows * depth * count, bytes_accessed=2 * depth * (2 * count + 4 * rows), transcendentals=0
        ),
    )(place_of, *tokens, *weight, *direction)


def sums_kernel(scalars, product, cur, prev, out):
    unit, coeff = scalars[0], scalars[1]
    p, c = product[...] * unit, cur[...]
    w = p - coeff * prev[...]
    rows = lax.broadcasted_iota(jnp.int32, out.shape, 0)
    table = jnp.zeros(out.shape, F32)
    for i, v in enumerate((c * p, c * c, w * w, w * c)):
        table = jnp.where(rows == i, jnp.sum(v), table)

    @pl.when(pl.program_id(0) == 0)
    def _():
        out[...] = jnp.zeros_like(out)

    out[...] += table


def sums_of(scalars, product, cur, prev):
    rows, depth = cur.shape
    block = pl.BlockSpec((rows // 4, depth), lambda i: (i, 0))
    return pl.pallas_call(
        sums_kernel,
        out_shape=jax.ShapeDtypeStruct((8, 128), F32),
        grid=(4,),
        in_specs=[pl.BlockSpec(memory_space=pltpu.SMEM), block, block, block],
        out_specs=pl.BlockSpec((8, 128), lambda i: (0, 0)),
        compiler_params=pltpu.CompilerParams(vmem_limit_bytes=32 * 2**20),
    )(scalars, product, cur, prev)


def step_kernel(entries, scalars, table, product, cur, prev, fresh, coefficients):
    unit, coeff = scalars[0], scalars[1]
    t = table[...]
    dot_cp, dot_cc, dot_ww, dot_wc = (t[i : i + 1, 0:1] for i in range(4))
    alpha = dot_cp / entries
    mean_sq = (dot_ww - 2.0 * alpha * dot_wc + alpha * alpha * dot_cc) / entries
    beta = jnp.sqrt(jnp.maximum(mean_sq, 0.0) + EPS_MEAN)
    resid = product[...] * unit - alpha * cur[...] - coeff * prev[...]
    fresh[...] = resid * (1.0 / beta)
    lane = lax.broadcasted_iota(jnp.int32, coefficients.shape, 1)
    coefficients[...] = jnp.where(lane == 0, alpha, beta)


def step_of(entries, scalars, table, product, cur, prev):
    rows, depth = cur.shape
    block = pl.BlockSpec((rows // 4, depth), lambda i: (i, 0))
    small = pl.BlockSpec((8, 128), lambda i: (0, 0))
    return pl.pallas_call(
        lambda *refs: step_kernel(entries, *refs),
        out_shape=[jax.ShapeDtypeStruct((rows, depth), F32), jax.ShapeDtypeStruct((8, 128), F32)],
        grid=(4,),
        in_specs=[pl.BlockSpec(memory_space=pltpu.SMEM), small, block, block, block],
        out_specs=[block, small],
        compiler_params=pltpu.CompilerParams(vmem_limit_bytes=32 * 2**20),
    )(scalars, table, product, cur, prev)


def curvature(hidden, tangent, sums, target, width, count):
    sums = sum_group(sums)
    squares, cross = sums[0], sums[1]
    scale = lax.rsqrt(squares / width + EPS_NORM)
    bound = jnp.sum(scale * scale * jnp.sqrt(sums[2])) * (PRODUCT_BOUND / count)
    bound = max_x(jnp.full((8, 128), bound, F32))
    power = two_to(HALF_BITS - 2.0, bound[0, 0])
    scale_dot = -(scale * scale * scale) * cross / width
    normed = hidden * scale
    normed_dot = tangent * scale + hidden * scale_dot
    sig, first, second = silu_terms(normed)
    error = normed * sig - target.astype(F32)
    grad_u = error * first / count
    grad_dot = (first * first + error * second) * normed_dot / count
    sums = sum_group(
        jnp.stack([jnp.sum(grad_u * hidden, 0), jnp.sum(grad_dot * hidden + grad_u * tangent, 0)])
    )
    inner = sums[0] / width
    inner_dot = sums[1] / width
    cube = scale * scale * scale
    result = (
        scale_dot * grad_u
        + scale * grad_dot
        - 3.0 * scale * scale * scale_dot * hidden * inner
        - cube * tangent * inner
        - cube * hidden * inner_dot
    )
    return (result * jnp.exp2(power)).astype(jnp.bfloat16), power, bound


def take(stack, index):
    return lax.dynamic_index_in_dim(stack, index, 0, keepdims=False)


def beside(own, axis):
    return lax.ppermute(own, axis, shift(4, 1)), lax.ppermute(own, axis, shift(4, 3))


def opposite(back, ahead, axis):
    half = back.shape[0] // 2
    return lax.ppermute(back[:half], axis, shift(4, 1)), lax.ppermute(ahead[half:], axis, shift(4, 3))


def over_z(own, x):
    quarter = own.shape[1] // 4
    return lax.ppermute(lax.dynamic_slice_in_dim(own, x * quarter, quarter, 1), "zh", xor(2, 1))


def swap_core(v):
    return lax.ppermute(v, "c", xor(2, 1))


def per_device(tokens, targets, weight, cur, prev, beta_prev):
    x, zl, zh = (lax.axis_index(n) for n in ("x", "zl", "zh"))
    z = zh * 4 + zl
    width, own = targets.shape
    rows, depth = weight.shape
    total = own * 256

    y, core = lax.axis_index("y"), lax.axis_index("c")
    direction = cur.astype(jnp.bfloat16)
    near = beside(tokens, "y")
    weight_part = over_z(weight, x)
    weight_near = beside(weight_part, "x")
    near, weight_near, direction_part = lax.optimization_barrier((near, weight_near, over_z(direction, x)))
    far = opposite(*near, "y")
    direction_near = beside(direction_part, "x")
    weight_far = opposite(*weight_near, "x")
    far, direction_near, weight_far = lax.optimization_barrier((far, direction_near, weight_far))
    direction_far = opposite(*direction_near, "x")
    pairs = [v for block in (tokens, *near) for v in (block, swap_core(block))]
    group = (*pairs, *far, *[swap_core(v) for v in far])
    blocks = targets.reshape(4, 2, 2, rows, own).transpose(0, 2, 1, 3, 4).reshape(8, 2 * rows, own)
    blocks, last = lax.optimization_barrier((blocks, group[-1]))
    group = (*group[:-1], last)
    columns = lax.all_to_all(blocks, ("y", "c"), split_axis=0, concat_axis=2, tiled=True)
    columns = columns.reshape(2 * rows, 8 * own)

    place_of = jnp.stack([y, (y + 3) % 4, (y + 1) % 4, (y + 2) % 4, x, core, zh])
    hidden, tangent, sums, gathered = project(
        place_of,
        group,
        (weight, weight_part, *weight_near, *weight_far),
        (direction, direction_part, *direction_near, *direction_far),
    )
    curv, power, bound = curvature(hidden, tangent, sums, columns, F32(width), F32(total))

    quarter, f16 = depth // 4, jnp.float16

    def partial(k):
        block = lax.dynamic_slice_in_dim(gathered, ((x + k) % 4) * quarter, quarter, 1)
        return jnp.dot(curv, block, preferred_element_type=F32)

    far = partial(2).astype(f16)
    up = lax.ppermute(far[:rows], "x", shift(4, 1))
    down = lax.ppermute(far[rows:], "x", shift(4, 3))
    near_up, near_down = partial(1), partial(3)
    near_up = jnp.concatenate([near_up[:rows] + up.astype(F32), near_up[rows:]])
    near_down = jnp.concatenate([near_down[:rows], near_down[rows:] + down.astype(F32)])
    up = lax.ppermute(near_up.astype(f16), "x", shift(4, 1))
    down = lax.ppermute(near_down.astype(f16), "x", shift(4, 3))
    share = partial(0) + up.astype(F32) + down.astype(F32)

    shared = two_to(HALF_BITS - 5.0, max_z(bound)[0, 0])
    unit = jnp.exp2(-shared)
    share = share.reshape(8, rows // 4, quarter) * jnp.exp2(shared - power)
    packed = share.astype(jnp.float16)
    piece = take(share, z)
    for k in (4, 3, 5, 2, 6, 1, 7):
        piece = piece + lax.ppermute(take(packed, (z + k) % 8), Z, zshift(k)).astype(F32)

    packed = piece.astype(jnp.float16)
    line = jnp.zeros((4,) + packed.shape, jnp.float16)
    line = lax.dynamic_update_index_in_dim(line, packed, zl, 0)
    for k in (3, 1, 2):
        got = lax.ppermute(packed, "zl", shift(4, k))
        line = lax.dynamic_update_index_in_dim(line, got, (zl - k) % 4, 0)
    product = lax.all_gather(line.reshape(rows, quarter), "x", axis=0, tiled=False)
    product = product.transpose(1, 0, 2).reshape(rows, depth).astype(F32)

    scalars = jnp.stack([unit, beta_prev[0]])
    table = sum_group(sums_of(scalars, product, cur, prev))
    table = table + lax.ppermute(table, "zh", xor(2, 1))
    fresh, coefficients = step_of(float(16 * rows * depth), scalars, table, product, cur, prev)
    return (fresh, coefficients[0, :2])


def solution(mesh):
    inner = Mesh(mesh.devices.reshape(4, 4, 4, 2, 2), ("zl", "x", "y", "zh", "c"))
    dp, shard = ("zl", "x"), ("y", "zh", "c")
    return jax.shard_map(
        per_device,
        mesh=inner,
        in_specs=(
            P(dp + shard, None),
            P(None, dp + shard),
            P(shard, None),
            P(shard, None),
            P(shard, None),
            P(),
        ),
        out_specs=(P(shard, None), P()),
        check_vma=False,
    )
```

```python
import jax
import jax.numpy as jnp
from jax import lax
from jax.experimental import pallas as pl
from jax.experimental.pallas import tpu as pltpu
from jax.sharding import Mesh, PartitionSpec as P

EPS_NORM = 1e-05
EPS_MEAN = 1e-06
PRODUCT_BOUND = 6.0 * 170.0
HALF_BITS = 15.0
Z = ("zl", "zh")
F32 = jnp.float32


def place(z):
    return (z % 4) * 2 + z // 4


def shift(n, k):
    return [(i, (i + k) % n) for i in range(n)]


def zshift(k):
    return [(place(i), place((i + k) % 8)) for i in range(8)]


def xor(n, k):
    return [(i, i ^ k) for i in range(n)]


def sum_group(v):
    v = v + lax.ppermute(v, "c", xor(2, 1))
    v = v + lax.ppermute(v, "y", xor(4, 1))
    return v + lax.ppermute(v, "y", xor(4, 3))


def max_x(v):
    for k in (1, 3):
        v = jnp.maximum(v, lax.ppermute(v, "x", xor(4, k)))
    return v


def max_z(v):
    for k in (1, 2, 4):
        v = jnp.maximum(v, lax.ppermute(v, Z, [(place(i), place(i ^ k)) for i in range(8)]))
    return v


def two_to(bits, bound):
    return jnp.clip(bits - jnp.ceil(jnp.log2(bound)), -100.0, 100.0)


def silu_terms(normed):
    sig = jax.nn.sigmoid(normed)
    first = sig * (1.0 + normed * (1.0 - sig))
    second = sig * (1.0 - sig) * (2.0 + normed * (1.0 - 2.0 * sig))
    return (sig, first, second)


def project_kernel(place_of, *refs):
    tokens, own_rows, eighths = refs[:10], refs[10:12], (refs[12:17], refs[17:22])
    hid, tan, sums, gathered = refs[22:26]
    left, tok, mat_sems, tok_sems, out_sems = refs[26:]
    i = pl.program_id(0)
    x, c, half, odd = (place_of[n] for n in (4, 5, 6, 7))
    rows, depth = own_rows[0].shape
    own, eighth = tokens[0].shape[0], depth // 8

    def mat_copies():
        bases = [[pl.multiple_of(2 * rows * m + h * rows, 16) for m in range(2)] for h in (half, 1 - half)]
        copies = [(own_rows[m], left.at[pl.ds(bases[0][m], rows), :]) for m in range(2)]
        for parity, parts in zip((odd, 1 - odd), eighths):
            for part, back, which in zip(parts, (0, 1, 3, 2, 2), ((0, 1), (0, 1), (0, 1), (0,), (1,))):
                at = pl.multiple_of((lax.rem(x + 4 - back, 4) * 2 + parity) * eighth, 128)
                for n, m in enumerate(which):
                    copies.append(
                        (part.at[pl.ds(n * rows, rows), :], left.at[pl.ds(bases[1][m], rows), pl.ds(at, eighth)])
                    )
        return [pltpu.make_async_copy(f, t, mat_sems.at[n]) for n, (f, t) in enumerate(copies)]

    def tok_copies(chunk):
        mine, theirs = pl.multiple_of(c * own, 16), pl.multiple_of((1 - c) * own, 16)
        if chunk < 3:
            pairs = ((tokens[2 * chunk], mine), (tokens[2 * chunk + 1], theirs))
        else:
            pairs = ((tokens[6], mine), (tokens[7], mine + own // 2), (tokens[8], theirs), (tokens[9], theirs + own // 2))
        return [
            pltpu.make_async_copy(
                ref, tok.at[chunk, pl.ds(pl.multiple_of(at, 16), ref.shape[0]), :], tok_sems.at[2 * chunk + n]
            )
            for n, (ref, at) in enumerate(pairs)
        ]

    def out_copy(chunk):
        at = pl.multiple_of(place_of[chunk] * 2 * own, 16)
        return pltpu.make_async_copy(tok.at[chunk], gathered.at[pl.ds(at, 2 * own), :], out_sems.at[chunk])

    @pl.when(i == 0)
    def _():
        for copy in mat_copies():
            copy.start()
        for chunk in range(4):
            for copy in tok_copies(chunk):
                copy.start()
        for copy in mat_copies():
            copy.wait()

    for chunk in range(4):

        @pl.when(i == chunk)
        def _():
            for copy in tok_copies(chunk):
                copy.wait()
            out_copy(chunk).start()

    both = lax.dot_general(
        left[...], tok[i], (((1,), (1,)), ((), ())), preferred_element_type=F32
    )
    h, t = both[: 2 * rows], both[2 * rows :]
    hid[...] = h
    tan[...] = t
    sums[...] = jnp.zeros_like(sums)
    sums[0:1, :] = jnp.sum(h * h, 0, keepdims=True)
    sums[1:2, :] = jnp.sum(h * t, 0, keepdims=True)
    sums[2:3, :] = jnp.sum(t * t, 0, keepdims=True)

    @pl.when(i == 3)
    def _():
        for chunk in range(4):
            out_copy(chunk).wait()


def project(place_of, tokens, own_rows, eighths):
    own, depth = tokens[0].shape
    rows = own_rows[0].shape[0]
    count, step = 8 * own, 2 * own
    held = pl.BlockSpec(memory_space=pl.ANY)
    out = pl.BlockSpec((2 * rows, step), lambda i, p: (0, p[i]))
    return pl.pallas_call(
        project_kernel,
        out_shape=[
            jax.ShapeDtypeStruct((2 * rows, count), F32),
            jax.ShapeDtypeStruct((2 * rows, count), F32),
            jax.ShapeDtypeStruct((8, count), F32),
            jax.ShapeDtypeStruct((count, depth), jnp.bfloat16),
        ],
        grid_spec=pltpu.PrefetchScalarGridSpec(
            num_scalar_prefetch=1,
            grid=(4,),
            in_specs=[held] * 22,
            out_specs=[out, out, pl.BlockSpec((8, step), lambda i, p: (0, p[i])), held],
            scratch_shapes=[
                pltpu.VMEM((4 * rows, depth), jnp.bfloat16),
                pltpu.VMEM((4, step, depth), jnp.bfloat16),
                pltpu.SemaphoreType.DMA((18,)),
                pltpu.SemaphoreType.DMA((10,)),
                pltpu.SemaphoreType.DMA((4,)),
            ],
        ),
        compiler_params=pltpu.CompilerParams(vmem_limit_bytes=50 * 2**20),
        cost_estimate=pl.CostEstimate(
            flops=8 * rows * depth * count, bytes_accessed=2 * depth * (2 * count + 4 * rows), transcendentals=0
        ),
    )(place_of, *tokens, *own_rows, *eighths)


def sums_kernel(scalars, product, cur, prev, out):
    unit, coeff = scalars[0], scalars[1]
    p, c = product[...] * unit, cur[...]
    w = p - coeff * prev[...]
    rows = lax.broadcasted_iota(jnp.int32, out.shape, 0)
    table = jnp.zeros(out.shape, F32)
    for i, v in enumerate((c * p, c * c, w * w, w * c)):
        table = jnp.where(rows == i, jnp.sum(v), table)

    @pl.when(pl.program_id(0) == 0)
    def _():
        out[...] = jnp.zeros_like(out)

    out[...] += table


def sums_of(scalars, product, cur, prev):
    rows, depth = cur.shape
    block = pl.BlockSpec((rows // 4, depth), lambda i: (i, 0))
    return pl.pallas_call(
        sums_kernel,
        out_shape=jax.ShapeDtypeStruct((8, 128), F32),
        grid=(4,),
        in_specs=[pl.BlockSpec(memory_space=pltpu.SMEM), block, block, block],
        out_specs=pl.BlockSpec((8, 128), lambda i: (0, 0)),
        compiler_params=pltpu.CompilerParams(vmem_limit_bytes=32 * 2**20),
    )(scalars, product, cur, prev)


def step_kernel(entries, scalars, table, product, cur, prev, fresh, coefficients):
    unit, coeff = scalars[0], scalars[1]
    t = table[...]
    dot_cp, dot_cc, dot_ww, dot_wc = (t[i : i + 1, 0:1] for i in range(4))
    alpha = dot_cp / entries
    mean_sq = (dot_ww - 2.0 * alpha * dot_wc + alpha * alpha * dot_cc) / entries
    beta = jnp.sqrt(jnp.maximum(mean_sq, 0.0) + EPS_MEAN)
    resid = product[...] * unit - alpha * cur[...] - coeff * prev[...]
    fresh[...] = resid * (1.0 / beta)
    lane = lax.broadcasted_iota(jnp.int32, coefficients.shape, 1)
    coefficients[...] = jnp.where(lane == 0, alpha, beta)


def step_of(entries, scalars, table, product, cur, prev):
    rows, depth = cur.shape
    block = pl.BlockSpec((rows // 4, depth), lambda i: (i, 0))
    small = pl.BlockSpec((8, 128), lambda i: (0, 0))
    return pl.pallas_call(
        lambda *refs: step_kernel(entries, *refs),
        out_shape=[jax.ShapeDtypeStruct((rows, depth), F32), jax.ShapeDtypeStruct((8, 128), F32)],
        grid=(4,),
        in_specs=[pl.BlockSpec(memory_space=pltpu.SMEM), small, block, block, block],
        out_specs=[block, small],
        compiler_params=pltpu.CompilerParams(vmem_limit_bytes=32 * 2**20),
    )(scalars, table, product, cur, prev)


def curvature(hidden, tangent, sums, target, width, count):
    sums = sum_group(sums)
    squares, cross = sums[0], sums[1]
    scale = lax.rsqrt(squares / width + EPS_NORM)
    bound = jnp.sum(scale * scale * jnp.sqrt(sums[2])) * (PRODUCT_BOUND / count)
    bound = max_z(max_x(jnp.full((8, 128), bound, F32)))
    power = two_to(HALF_BITS - 5.0, bound[0, 0])
    scale_dot = -(scale * scale * scale) * cross / width
    normed = hidden * scale
    normed_dot = tangent * scale + hidden * scale_dot
    sig, first, second = silu_terms(normed)
    error = normed * sig - target.astype(F32)
    grad_u = error * first / count
    grad_dot = (first * first + error * second) * normed_dot / count
    sums = sum_group(
        jnp.stack([jnp.sum(grad_u * hidden, 0), jnp.sum(grad_dot * hidden + grad_u * tangent, 0)])
    )
    inner = sums[0] / width
    inner_dot = sums[1] / width
    cube = scale * scale * scale
    result = (
        scale_dot * grad_u
        + scale * grad_dot
        - 3.0 * scale * scale * scale_dot * hidden * inner
        - cube * tangent * inner
        - cube * hidden * inner_dot
    )
    return result.astype(jnp.bfloat16), power


def take(stack, index):
    return lax.dynamic_index_in_dim(stack, index, 0, keepdims=False)


def beside(own, axis):
    return lax.ppermute(own, axis, shift(4, 1)), lax.ppermute(own, axis, shift(4, 3))


def opposite(back, ahead, axis):
    half = back.shape[0] // 2
    return lax.ppermute(back[:half], axis, shift(4, 1)), lax.ppermute(ahead[half:], axis, shift(4, 3))


def swap_core(v):
    return lax.ppermute(v, "c", xor(2, 1))


def per_device(tokens, targets, weight, cur, prev, beta_prev):
    x, zl, zh = (lax.axis_index(n) for n in ("x", "zl", "zh"))
    z = zh * 4 + zl
    width, own = targets.shape
    rows, depth = weight.shape
    total = own * 256

    y, core = lax.axis_index("y"), lax.axis_index("c")
    direction = cur.astype(jnp.bfloat16)
    near = beside(tokens, "y")
    odd, eighth = zl % 2, depth // 8
    at = (2 * x + odd) * eighth
    first = jnp.concatenate(
        [lax.dynamic_slice_in_dim(v, at, eighth, 1).astype(jnp.bfloat16) for v in (weight, cur)]
    )
    first = lax.ppermute(first, "zh", xor(2, 1))
    second = lax.ppermute(first, "zl", xor(4, 1))
    first_near = beside(first, "x")
    near, first_near, second = lax.optimization_barrier((near, first_near, second))
    far = opposite(*near, "y")
    second_near = beside(second, "x")
    first_far = opposite(*first_near, "x")
    far, second_near, first_far = lax.optimization_barrier((far, second_near, first_far))
    second_far = opposite(*second_near, "x")
    pairs = [v for block in (tokens, *near) for v in (block, swap_core(block))]
    group = (*pairs, *far, *[swap_core(v) for v in far])
    blocks = targets.reshape(4, 2, 2, rows, own).transpose(0, 2, 1, 3, 4).reshape(8, 2 * rows, own)
    blocks, last = lax.optimization_barrier((blocks, group[-1]))
    group = (*group[:-1], last)
    columns = lax.all_to_all(blocks, ("y", "c"), split_axis=0, concat_axis=2, tiled=True)
    columns = columns.reshape(2 * rows, 8 * own)

    place_of = jnp.stack([y, (y + 3) % 4, (y + 1) % 4, (y + 2) % 4, x, core, zh, odd])
    hidden, tangent, sums, gathered = project(
        place_of,
        group,
        (weight, direction),
        (first, *first_near, *first_far, second, *second_near, *second_far),
    )
    curv, power = curvature(hidden, tangent, sums, columns, F32(width), F32(total))

    quarter, f16 = depth // 4, jnp.float16

    def partial(k):
        block = lax.dynamic_slice_in_dim(gathered, ((x + k) % 4) * quarter, quarter, 1)
        return jnp.dot(curv, block, preferred_element_type=F32) * jnp.exp2(power)

    far = partial(2).astype(f16)
    up = lax.ppermute(far[:rows], "x", shift(4, 1))
    down = lax.ppermute(far[rows:], "x", shift(4, 3))
    near_up, near_down = partial(1), partial(3)
    near_up = jnp.concatenate([near_up[:rows] + up.astype(F32), near_up[rows:]])
    near_down = jnp.concatenate([near_down[:rows], near_down[rows:] + down.astype(F32)])
    up = lax.ppermute(near_up.astype(f16), "x", shift(4, 1))
    down = lax.ppermute(near_down.astype(f16), "x", shift(4, 3))
    share = partial(0) + up.astype(F32) + down.astype(F32)

    unit = jnp.exp2(-power)
    share = share.reshape(8, rows // 4, quarter)
    packed = share.astype(jnp.float16)
    piece = take(share, z)
    for k in (4, 3, 5, 2, 6, 1, 7):
        piece = piece + lax.ppermute(take(packed, (z + k) % 8), Z, zshift(k)).astype(F32)

    packed = piece.astype(jnp.float16)
    line = jnp.zeros((4,) + packed.shape, jnp.float16)
    line = lax.dynamic_update_index_in_dim(line, packed, zl, 0)
    for k in (3, 1, 2):
        got = lax.ppermute(packed, "zl", shift(4, k))
        line = lax.dynamic_update_index_in_dim(line, got, (zl - k) % 4, 0)
    product = lax.all_gather(line.reshape(rows, quarter), "x", axis=0, tiled=False)
    product = product.transpose(1, 0, 2).reshape(rows, depth).astype(F32)

    scalars = jnp.stack([unit, beta_prev[0]])
    table = sum_group(sums_of(scalars, product, cur, prev))
    table = table + lax.ppermute(table, "zh", xor(2, 1))
    fresh, coefficients = step_of(float(16 * rows * depth), scalars, table, product, cur, prev)
    return (fresh, coefficients[0, :2])


def solution(mesh):
    inner = Mesh(mesh.devices.reshape(4, 4, 4, 2, 2), ("zl", "x", "y", "zh", "c"))
    dp, shard = ("zl", "x"), ("y", "zh", "c")
    return jax.shard_map(
        per_device,
        mesh=inner,
        in_specs=(
            P(dp + shard, None),
            P(None, dp + shard),
            P(shard, None),
            P(shard, None),
            P(shard, None),
            P(),
        ),
        out_specs=(P(shard, None), P()),
        check_vma=False,
    )
```

```python
import jax
import jax.numpy as jnp
from jax import lax
from jax.experimental import pallas as pl
from jax.experimental.pallas import tpu as pltpu
from jax.sharding import Mesh, PartitionSpec as P

EPS_NORM = 1e-05
EPS_MEAN = 1e-06
PRODUCT_BOUND = 6.0 * 170.0
HALF_BITS = 15.0
Z = ("zl", "zh")
F32 = jnp.float32


def place(z):
    return (z % 4) * 2 + z // 4


def shift(n, k):
    return [(i, (i + k) % n) for i in range(n)]


def zshift(k):
    return [(place(i), place((i + k) % 8)) for i in range(8)]


def xor(n, k):
    return [(i, i ^ k) for i in range(n)]


def sum_group(v):
    v = v + lax.ppermute(v, "c", xor(2, 1))
    v = v + lax.ppermute(v, "y", xor(4, 1))
    return v + lax.ppermute(v, "y", xor(4, 3))


def max_x(v):
    for k in (1, 3):
        v = jnp.maximum(v, lax.ppermute(v, "x", xor(4, k)))
    return v


def max_z(v):
    for k in (1, 2, 4):
        v = jnp.maximum(v, lax.ppermute(v, Z, [(place(i), place(i ^ k)) for i in range(8)]))
    return v


def two_to(bits, bound):
    return jnp.clip(bits - jnp.ceil(jnp.log2(bound)), -100.0, 100.0)


def silu_terms(normed):
    sig = jax.nn.sigmoid(normed)
    first = sig * (1.0 + normed * (1.0 - sig))
    second = sig * (1.0 - sig) * (2.0 + normed * (1.0 - 2.0 * sig))
    return (sig, first, second)


def project_kernel(place_of, *refs):
    tokens, mats = refs[:10], (refs[10:16], refs[16:22])
    hid, tan, sums, gathered = refs[22:26]
    left, tok, mat_sems, tok_sems, out_sems = refs[26:]
    i = pl.program_id(0)
    x, c, half = place_of[4], place_of[5], place_of[6]
    rows, depth = mats[0][0].shape
    own, quarter = tokens[0].shape[0], depth // 4
    own_at = pl.multiple_of(half * rows, 16)
    other_at = (1 - half) * rows

    def mat_copies():
        copies = []
        for m, parts in enumerate(mats):
            base = 2 * rows * m
            copies.append((parts[0], left.at[pl.ds(pl.multiple_of(base + own_at, 16), rows), :]))
            for part, back, row in zip(parts[1:], (0, 1, 3, 2, 2), (0, 0, 0, 0, rows // 2)):
                at = pl.multiple_of(lax.rem(x + 4 - back, 4) * quarter, 128)
                place = pl.multiple_of(base + other_at + row, 16)
                copies.append((part, left.at[pl.ds(place, part.shape[0]), pl.ds(at, quarter)]))
        return [pltpu.make_async_copy(f, t, mat_sems.at[n]) for n, (f, t) in enumerate(copies)]

    def tok_copies(chunk):
        mine, theirs = pl.multiple_of(c * own, 16), pl.multiple_of((1 - c) * own, 16)
        if chunk < 3:
            pairs = ((tokens[2 * chunk], mine), (tokens[2 * chunk + 1], theirs))
        else:
            pairs = ((tokens[6], mine), (tokens[7], mine + own // 2), (tokens[8], theirs), (tokens[9], theirs + own // 2))
        return [
            pltpu.make_async_copy(
                ref, tok.at[chunk, pl.ds(pl.multiple_of(at, 16), ref.shape[0]), :], tok_sems.at[2 * chunk + n]
            )
            for n, (ref, at) in enumerate(pairs)
        ]

    def out_copy(chunk):
        at = pl.multiple_of(place_of[chunk] * 2 * own, 16)
        return pltpu.make_async_copy(tok.at[chunk], gathered.at[pl.ds(at, 2 * own), :], out_sems.at[chunk])

    @pl.when(i == 0)
    def _():
        for copy in mat_copies():
            copy.start()
        for chunk in range(4):
            for copy in tok_copies(chunk):
                copy.start()
        for copy in mat_copies():
            copy.wait()

    for chunk in range(4):

        @pl.when(i == chunk)
        def _():
            for copy in tok_copies(chunk):
                copy.wait()
            out_copy(chunk).start()

    both = lax.dot_general(
        left[...], tok[i], (((1,), (1,)), ((), ())), preferred_element_type=F32
    )
    h, t = both[: 2 * rows], both[2 * rows :]
    hid[...] = h
    tan[...] = t
    sums[...] = jnp.zeros_like(sums)
    sums[0:1, :] = jnp.sum(h * h, 0, keepdims=True)
    sums[1:2, :] = jnp.sum(h * t, 0, keepdims=True)
    sums[2:3, :] = jnp.sum(t * t, 0, keepdims=True)

    @pl.when(i == 3)
    def _():
        for chunk in range(4):
            out_copy(chunk).wait()


def project(place_of, tokens, weight, direction):
    own, depth = tokens[0].shape
    rows = weight[0].shape[0]
    count, step = 8 * own, 2 * own
    held = pl.BlockSpec(memory_space=pl.ANY)
    out = pl.BlockSpec((2 * rows, step), lambda i, p: (0, p[i]))
    return pl.pallas_call(
        project_kernel,
        out_shape=[
            jax.ShapeDtypeStruct((2 * rows, count), F32),
            jax.ShapeDtypeStruct((2 * rows, count), F32),
            jax.ShapeDtypeStruct((8, count), F32),
            jax.ShapeDtypeStruct((count, depth), jnp.bfloat16),
        ],
        grid_spec=pltpu.PrefetchScalarGridSpec(
            num_scalar_prefetch=1,
            grid=(4,),
            in_specs=[held] * 22,
            out_specs=[out, out, pl.BlockSpec((8, step), lambda i, p: (0, p[i])), held],
            scratch_shapes=[
                pltpu.VMEM((4 * rows, depth), jnp.bfloat16),
                pltpu.VMEM((4, step, depth), jnp.bfloat16),
                pltpu.SemaphoreType.DMA((12,)),
                pltpu.SemaphoreType.DMA((10,)),
                pltpu.SemaphoreType.DMA((4,)),
            ],
        ),
        compiler_params=pltpu.CompilerParams(vmem_limit_bytes=26 * 2**20),
        cost_estimate=pl.CostEstimate(
            flops=8 * rows * depth * count, bytes_accessed=2 * depth * (2 * count + 4 * rows), transcendentals=0
        ),
    )(place_of, *tokens, *weight, *direction)


def sums_kernel(scalars, product, cur, prev, out):
    unit, coeff = scalars[0], scalars[1]
    p, c = product[...] * unit, cur[...]
    w = p - coeff * prev[...]
    rows = lax.broadcasted_iota(jnp.int32, out.shape, 0)
    table = jnp.zeros(out.shape, F32)
    for i, v in enumerate((c * p, c * c, w * w, w * c)):
        table = jnp.where(rows == i, jnp.sum(v), table)

    @pl.when(pl.program_id(0) == 0)
    def _():
        out[...] = jnp.zeros_like(out)

    out[...] += table


def sums_of(scalars, product, cur, prev):
    rows, depth = cur.shape
    block = pl.BlockSpec((rows // 4, depth), lambda i: (i, 0))
    return pl.pallas_call(
        sums_kernel,
        out_shape=jax.ShapeDtypeStruct((8, 128), F32),
        grid=(4,),
        in_specs=[pl.BlockSpec(memory_space=pltpu.SMEM), block, block, block],
        out_specs=pl.BlockSpec((8, 128), lambda i: (0, 0)),
        compiler_params=pltpu.CompilerParams(vmem_limit_bytes=32 * 2**20),
    )(scalars, product, cur, prev)


def step_kernel(entries, scalars, table, product, cur, prev, fresh, coefficients):
    unit, coeff = scalars[0], scalars[1]
    t = table[...]
    dot_cp, dot_cc, dot_ww, dot_wc = (t[i : i + 1, 0:1] for i in range(4))
    alpha = dot_cp / entries
    mean_sq = (dot_ww - 2.0 * alpha * dot_wc + alpha * alpha * dot_cc) / entries
    beta = jnp.sqrt(jnp.maximum(mean_sq, 0.0) + EPS_MEAN)
    resid = product[...] * unit - alpha * cur[...] - coeff * prev[...]
    fresh[...] = resid * (1.0 / beta)
    lane = lax.broadcasted_iota(jnp.int32, coefficients.shape, 1)
    coefficients[...] = jnp.where(lane == 0, alpha, beta)


def step_of(entries, scalars, table, product, cur, prev):
    rows, depth = cur.shape
    block = pl.BlockSpec((rows // 4, depth), lambda i: (i, 0))
    small = pl.BlockSpec((8, 128), lambda i: (0, 0))
    return pl.pallas_call(
        lambda *refs: step_kernel(entries, *refs),
        out_shape=[jax.ShapeDtypeStruct((rows, depth), F32), jax.ShapeDtypeStruct((8, 128), F32)],
        grid=(4,),
        in_specs=[pl.BlockSpec(memory_space=pltpu.SMEM), small, block, block, block],
        out_specs=[block, small],
        compiler_params=pltpu.CompilerParams(vmem_limit_bytes=32 * 2**20),
    )(scalars, table, product, cur, prev)


def curvature(hidden, tangent, sums, target, width, count):
    sums = sum_group(sums)
    squares, cross = sums[0], sums[1]
    scale = lax.rsqrt(squares / width + EPS_NORM)
    bound = jnp.sum(scale * scale * jnp.sqrt(sums[2])) * (PRODUCT_BOUND / count)
    bound = max_x(jnp.full((8, 128), bound, F32))
    power = two_to(HALF_BITS - 2.0, bound[0, 0])
    scale_dot = -(scale * scale * scale) * cross / width
    normed = hidden * scale
    normed_dot = tangent * scale + hidden * scale_dot
    sig, first, second = silu_terms(normed)
    error = normed * sig - target.astype(F32)
    grad_u = error * first / count
    grad_dot = (first * first + error * second) * normed_dot / count
    sums = sum_group(
        jnp.stack([jnp.sum(grad_u * hidden, 0), jnp.sum(grad_dot * hidden + grad_u * tangent, 0)])
    )
    inner = sums[0] / width
    inner_dot = sums[1] / width
    cube = scale * scale * scale
    result = (
        scale_dot * grad_u
        + scale * grad_dot
        - 3.0 * scale * scale * scale_dot * hidden * inner
        - cube * tangent * inner
        - cube * hidden * inner_dot
    )
    return (result * jnp.exp2(power)).astype(jnp.bfloat16), power, bound


def take(stack, index):
    return lax.dynamic_index_in_dim(stack, index, 0, keepdims=False)


def beside(own, axis):
    return lax.ppermute(own, axis, shift(4, 1)), lax.ppermute(own, axis, shift(4, 3))


def opposite(back, ahead, axis):
    half = back.shape[0] // 2
    return lax.ppermute(back[:half], axis, shift(4, 1)), lax.ppermute(ahead[half:], axis, shift(4, 3))


def over_z(own, x):
    quarter = own.shape[1] // 4
    return lax.ppermute(lax.dynamic_slice_in_dim(own, x * quarter, quarter, 1), "zh", xor(2, 1))


def swap_core(v):
    return lax.ppermute(v, "c", xor(2, 1))


def per_device(tokens, targets, weight, cur, prev, beta_prev):
    x, zl, zh = (lax.axis_index(n) for n in ("x", "zl", "zh"))
    z = zh * 4 + zl
    width, own = targets.shape
    rows, depth = weight.shape
    total = own * 256

    y, core = lax.axis_index("y"), lax.axis_index("c")
    direction = cur.astype(jnp.bfloat16)
    near = beside(tokens, "y")
    weight_part = over_z(weight, x)
    weight_near = beside(weight_part, "x")
    direction_part = over_z(direction, x)
    near, weight_near = lax.optimization_barrier((near, weight_near))
    far = opposite(*near, "y")
    weight_far = opposite(*weight_near, "x")
    direction_part, weight_far = lax.optimization_barrier((direction_part, weight_far))
    direction_near = beside(direction_part, "x")
    far = (*far, *[swap_core(v) for v in far])
    far, direction_near = lax.optimization_barrier((far, direction_near))
    direction_far = opposite(*direction_near, "x")
    pairs = [v for block in (tokens, *near) for v in (block, swap_core(block))]
    group = (*pairs, *far)
    blocks = targets.reshape(4, 2, 2, rows, own).transpose(0, 2, 1, 3, 4).reshape(8, 2 * rows, own)
    blocks, last = lax.optimization_barrier((blocks, group[7]))
    group = (*group[:7], last, *group[8:])
    columns = lax.all_to_all(blocks, ("y", "c"), split_axis=0, concat_axis=2, tiled=True)
    columns = columns.reshape(2 * rows, 8 * own)

    place_of = jnp.stack([y, (y + 3) % 4, (y + 1) % 4, (y + 2) % 4, x, core, zh])
    hidden, tangent, sums, gathered = project(
        place_of,
        group,
        (weight, weight_part, *weight_near, *weight_far),
        (direction, direction_part, *direction_near, *direction_far),
    )
    curv, power, bound = curvature(hidden, tangent, sums, columns, F32(width), F32(total))

    quarter, f16 = depth // 4, jnp.float16

    def partial(k):
        block = lax.dynamic_slice_in_dim(gathered, ((x + k) % 4) * quarter, quarter, 1)
        return jnp.dot(curv, block, preferred_element_type=F32)

    far = partial(2).astype(f16)
    up = lax.ppermute(far[:rows], "x", shift(4, 1))
    down = lax.ppermute(far[rows:], "x", shift(4, 3))
    near_up, near_down = partial(1), partial(3)
    near_up = jnp.concatenate([near_up[:rows] + up.astype(F32), near_up[rows:]])
    near_down = jnp.concatenate([near_down[:rows], near_down[rows:] + down.astype(F32)])
    up = lax.ppermute(near_up.astype(f16), "x", shift(4, 1))
    down = lax.ppermute(near_down.astype(f16), "x", shift(4, 3))
    share = partial(0) + up.astype(F32) + down.astype(F32)

    shared = two_to(HALF_BITS - 5.0, max_z(bound)[0, 0])
    unit = jnp.exp2(-shared)
    share = share.reshape(8, rows // 4, quarter) * jnp.exp2(shared - power)
    packed = share.astype(jnp.float16)
    piece = take(share, z)
    for k in (4, 3, 5, 2, 6, 1, 7):
        piece = piece + lax.ppermute(take(packed, (z + k) % 8), Z, zshift(k)).astype(F32)

    packed = piece.astype(jnp.float16)
    line = jnp.zeros((4,) + packed.shape, jnp.float16)
    line = lax.dynamic_update_index_in_dim(line, packed, zl, 0)
    for k in (3, 1, 2):
        got = lax.ppermute(packed, "zl", shift(4, k))
        line = lax.dynamic_update_index_in_dim(line, got, (zl - k) % 4, 0)
    product = lax.all_gather(line.reshape(rows, quarter), "x", axis=0, tiled=False)
    product = product.transpose(1, 0, 2).reshape(rows, depth).astype(F32)

    scalars = jnp.stack([unit, beta_prev[0]])
    table = sum_group(sums_of(scalars, product, cur, prev))
    table = table + lax.ppermute(table, "zh", xor(2, 1))
    fresh, coefficients = step_of(float(16 * rows * depth), scalars, table, product, cur, prev)
    return (fresh, coefficients[0, :2])


def solution(mesh):
    inner = Mesh(mesh.devices.reshape(4, 4, 4, 2, 2), ("zl", "x", "y", "zh", "c"))
    dp, shard = ("zl", "x"), ("y", "zh", "c")
    return jax.shard_map(
        per_device,
        mesh=inner,
        in_specs=(
            P(dp + shard, None),
            P(None, dp + shard),
            P(shard, None),
            P(shard, None),
            P(shard, None),
            P(),
        ),
        out_specs=(P(shard, None), P()),
        check_vma=False,
    )
```

```python
import jax
import jax.numpy as jnp
from jax import lax
from jax.experimental import pallas as pl
from jax.experimental.pallas import tpu as pltpu
from jax.sharding import Mesh, PartitionSpec as P

EPS_NORM = 1e-05
EPS_MEAN = 1e-06
PRODUCT_BOUND = 6.0 * 170.0
HALF_BITS = 15.0
Z = ("zl", "zh")
F32 = jnp.float32


def place(z):
    return (z % 4) * 2 + z // 4


def shift(n, k):
    return [(i, (i + k) % n) for i in range(n)]


def zshift(k):
    return [(place(i), place((i + k) % 8)) for i in range(8)]


def xor(n, k):
    return [(i, i ^ k) for i in range(n)]


def sum_group(v):
    v = v + lax.ppermute(v, "c", xor(2, 1))
    v = v + lax.ppermute(v, "y", xor(4, 1))
    return v + lax.ppermute(v, "y", xor(4, 3))


def max_x(v):
    for k in (1, 3):
        v = jnp.maximum(v, lax.ppermute(v, "x", xor(4, k)))
    return v


def max_z(v):
    for k in (1, 2, 4):
        v = jnp.maximum(v, lax.ppermute(v, Z, [(place(i), place(i ^ k)) for i in range(8)]))
    return v


def two_to(bits, bound):
    return jnp.clip(bits - jnp.ceil(jnp.log2(bound)), -100.0, 100.0)


def silu_terms(normed):
    sig = jax.nn.sigmoid(normed)
    first = sig * (1.0 + normed * (1.0 - sig))
    second = sig * (1.0 - sig) * (2.0 + normed * (1.0 - 2.0 * sig))
    return (sig, first, second)


def project_kernel(place_of, *refs):
    tokens, mats = refs[:10], (refs[10:16], refs[16:22])
    hid, tan, sums, gathered = refs[22:26]
    left, tok, mat_sems, tok_sems, out_sems = refs[26:]
    i = pl.program_id(0)
    x, c, half = place_of[4], place_of[5], place_of[6]
    rows, depth = mats[0][0].shape
    own, quarter = tokens[0].shape[0], depth // 4
    own_at = pl.multiple_of(half * rows, 16)
    other_at = (1 - half) * rows

    def mat_copies():
        copies = []
        for m, parts in enumerate(mats):
            base = 2 * rows * m
            copies.append((parts[0], left.at[pl.ds(pl.multiple_of(base + own_at, 16), rows), :]))
            for part, back, row in zip(parts[1:], (0, 1, 3, 2, 2), (0, 0, 0, 0, rows // 2)):
                at = pl.multiple_of(lax.rem(x + 4 - back, 4) * quarter, 128)
                place = pl.multiple_of(base + other_at + row, 16)
                copies.append((part, left.at[pl.ds(place, part.shape[0]), pl.ds(at, quarter)]))
        return [pltpu.make_async_copy(f, t, mat_sems.at[n]) for n, (f, t) in enumerate(copies)]

    def tok_copies(chunk):
        mine, theirs = pl.multiple_of(c * own, 16), pl.multiple_of((1 - c) * own, 16)
        if chunk < 3:
            pairs = ((tokens[2 * chunk], mine), (tokens[2 * chunk + 1], theirs))
        else:
            pairs = ((tokens[6], mine), (tokens[7], mine + own // 2), (tokens[8], theirs), (tokens[9], theirs + own // 2))
        return [
            pltpu.make_async_copy(
                ref, tok.at[chunk, pl.ds(pl.multiple_of(at, 16), ref.shape[0]), :], tok_sems.at[2 * chunk + n]
            )
            for n, (ref, at) in enumerate(pairs)
        ]

    def out_copy(chunk):
        at = pl.multiple_of(place_of[chunk] * 2 * own, 16)
        return pltpu.make_async_copy(tok.at[chunk], gathered.at[pl.ds(at, 2 * own), :], out_sems.at[chunk])

    @pl.when(i == 0)
    def _():
        for copy in mat_copies():
            copy.start()
        for chunk in range(4):
            for copy in tok_copies(chunk):
                copy.start()
        for copy in mat_copies():
            copy.wait()

    for chunk in range(4):

        @pl.when(i == chunk)
        def _():
            for copy in tok_copies(chunk):
                copy.wait()
            out_copy(chunk).start()

    both = lax.dot_general(
        left[...], tok[i], (((1,), (1,)), ((), ())), preferred_element_type=F32
    )
    h, t = both[: 2 * rows], both[2 * rows :]
    hid[...] = h
    tan[...] = t
    sums[...] = jnp.zeros_like(sums)
    sums[0:1, :] = jnp.sum(h * h, 0, keepdims=True)
    sums[1:2, :] = jnp.sum(h * t, 0, keepdims=True)
    sums[2:3, :] = jnp.sum(t * t, 0, keepdims=True)

    @pl.when(i == 3)
    def _():
        for chunk in range(4):
            out_copy(chunk).wait()


def project(place_of, tokens, weight, direction):
    own, depth = tokens[0].shape
    rows = weight[0].shape[0]
    count, step = 8 * own, 2 * own
    held = pl.BlockSpec(memory_space=pl.ANY)
    out = pl.BlockSpec((2 * rows, step), lambda i, p: (0, p[i]))
    return pl.pallas_call(
        project_kernel,
        out_shape=[
            jax.ShapeDtypeStruct((2 * rows, count), F32),
            jax.ShapeDtypeStruct((2 * rows, count), F32),
            jax.ShapeDtypeStruct((8, count), F32),
            jax.ShapeDtypeStruct((count, depth), jnp.bfloat16),
        ],
        grid_spec=pltpu.PrefetchScalarGridSpec(
            num_scalar_prefetch=1,
            grid=(4,),
            in_specs=[held] * 22,
            out_specs=[out, out, pl.BlockSpec((8, step), lambda i, p: (0, p[i])), held],
            scratch_shapes=[
                pltpu.VMEM((4 * rows, depth), jnp.bfloat16),
                pltpu.VMEM((4, step, depth), jnp.bfloat16),
                pltpu.SemaphoreType.DMA((12,)),
                pltpu.SemaphoreType.DMA((10,)),
                pltpu.SemaphoreType.DMA((4,)),
            ],
        ),
        compiler_params=pltpu.CompilerParams(vmem_limit_bytes=60 * 2**20),
        cost_estimate=pl.CostEstimate(
            flops=8 * rows * depth * count, bytes_accessed=2 * depth * (2 * count + 4 * rows), transcendentals=0
        ),
    )(place_of, *tokens, *weight, *direction)


def sums_kernel(scalars, product, cur, prev, out):
    unit, coeff = scalars[0], scalars[1]
    p, c = product[...] * unit, cur[...]
    w = p - coeff * prev[...]
    rows = lax.broadcasted_iota(jnp.int32, out.shape, 0)
    table = jnp.zeros(out.shape, F32)
    for i, v in enumerate((c * p, c * c, w * w, w * c)):
        table = jnp.where(rows == i, jnp.sum(v), table)

    @pl.when(pl.program_id(0) == 0)
    def _():
        out[...] = jnp.zeros_like(out)

    out[...] += table


def sums_of(scalars, product, cur, prev):
    rows, depth = cur.shape
    block = pl.BlockSpec((rows // 4, depth), lambda i: (i, 0))
    return pl.pallas_call(
        sums_kernel,
        out_shape=jax.ShapeDtypeStruct((8, 128), F32),
        grid=(4,),
        in_specs=[pl.BlockSpec(memory_space=pltpu.SMEM), block, block, block],
        out_specs=pl.BlockSpec((8, 128), lambda i: (0, 0)),
        compiler_params=pltpu.CompilerParams(vmem_limit_bytes=60 * 2**20),
    )(scalars, product, cur, prev)


def step_kernel(entries, scalars, table, product, cur, prev, fresh, coefficients):
    unit, coeff = scalars[0], scalars[1]
    t = table[...]
    dot_cp, dot_cc, dot_ww, dot_wc = (t[i : i + 1, 0:1] for i in range(4))
    alpha = dot_cp / entries
    mean_sq = (dot_ww - 2.0 * alpha * dot_wc + alpha * alpha * dot_cc) / entries
    beta = jnp.sqrt(jnp.maximum(mean_sq, 0.0) + EPS_MEAN)
    resid = product[...] * unit - alpha * cur[...] - coeff * prev[...]
    fresh[...] = resid * (1.0 / beta)
    lane = lax.broadcasted_iota(jnp.int32, coefficients.shape, 1)
    coefficients[...] = jnp.where(lane == 0, alpha, beta)


def step_of(entries, scalars, table, product, cur, prev):
    rows, depth = cur.shape
    block = pl.BlockSpec((rows // 4, depth), lambda i: (i, 0))
    small = pl.BlockSpec((8, 128), lambda i: (0, 0))
    return pl.pallas_call(
        lambda *refs: step_kernel(entries, *refs),
        out_shape=[jax.ShapeDtypeStruct((rows, depth), F32), jax.ShapeDtypeStruct((8, 128), F32)],
        grid=(4,),
        in_specs=[pl.BlockSpec(memory_space=pltpu.SMEM), small, block, block, block],
        out_specs=[block, small],
        compiler_params=pltpu.CompilerParams(vmem_limit_bytes=32 * 2**20),
    )(scalars, table, product, cur, prev)


def curvature(hidden, tangent, sums, target, width, count):
    sums = sum_group(sums)
    squares, cross = sums[0], sums[1]
    scale = lax.rsqrt(squares / width + EPS_NORM)
    bound = jnp.sum(scale * scale * jnp.sqrt(sums[2])) * (PRODUCT_BOUND / count)
    bound = max_x(jnp.full((8, 128), bound, F32))
    power = two_to(HALF_BITS - 2.0, bound[0, 0])
    scale_dot = -(scale * scale * scale) * cross / width
    normed = hidden * scale
    normed_dot = tangent * scale + hidden * scale_dot
    sig, first, second = silu_terms(normed)
    error = normed * sig - target.astype(F32)
    grad_u = error * first / count
    grad_dot = (first * first + error * second) * normed_dot / count
    sums = sum_group(
        jnp.stack([jnp.sum(grad_u * hidden, 0), jnp.sum(grad_dot * hidden + grad_u * tangent, 0)])
    )
    inner = sums[0] / width
    inner_dot = sums[1] / width
    cube = scale * scale * scale
    result = (
        scale_dot * grad_u
        + scale * grad_dot
        - 3.0 * scale * scale * scale_dot * hidden * inner
        - cube * tangent * inner
        - cube * hidden * inner_dot
    )
    return (result * jnp.exp2(power)).astype(jnp.bfloat16), power, bound


def take(stack, index):
    return lax.dynamic_index_in_dim(stack, index, 0, keepdims=False)


def beside(own, axis):
    return lax.ppermute(own, axis, shift(4, 1)), lax.ppermute(own, axis, shift(4, 3))


def opposite(back, ahead, axis):
    half = back.shape[0] // 2
    return lax.ppermute(back[:half], axis, shift(4, 1)), lax.ppermute(ahead[half:], axis, shift(4, 3))


def over_z(own, x):
    quarter = own.shape[1] // 4
    return lax.ppermute(lax.dynamic_slice_in_dim(own, x * quarter, quarter, 1), "zh", xor(2, 1))


def swap_core(v):
    return lax.ppermute(v, "c", xor(2, 1))


def per_device(tokens, targets, weight, cur, prev, beta_prev):
    x, zl, zh = (lax.axis_index(n) for n in ("x", "zl", "zh"))
    z = zh * 4 + zl
    width, own = targets.shape
    rows, depth = weight.shape
    total = own * 256

    y, core = lax.axis_index("y"), lax.axis_index("c")
    direction = cur.astype(jnp.bfloat16)
    near = beside(tokens, "y")
    weight_part = over_z(weight, x)
    weight_near = beside(weight_part, "x")
    blocks = targets.reshape(4, 2, 2, rows, own).transpose(0, 2, 1, 3, 4).reshape(8, 2 * rows, own)
    columns = lax.all_to_all(blocks, ("y", "c"), split_axis=0, concat_axis=2, tiled=True)
    columns = columns.reshape(2 * rows, 8 * own)
    near, weight_near, direction_part, columns = lax.optimization_barrier(
        (near, weight_near, over_z(direction, x), columns)
    )
    far = opposite(*near, "y")
    direction_near = beside(direction_part, "x")
    weight_far = opposite(*weight_near, "x")
    far, direction_near, weight_far = lax.optimization_barrier((far, direction_near, weight_far))
    direction_far = opposite(*direction_near, "x")
    pairs = [v for block in (tokens, *near) for v in (block, swap_core(block))]
    group = (*pairs, *far, *[swap_core(v) for v in far])
    place_of = jnp.stack([y, (y + 3) % 4, (y + 1) % 4, (y + 2) % 4, x, core, zh])
    hidden, tangent, sums, gathered = project(
        place_of,
        group,
        (weight, weight_part, *weight_near, *weight_far),
        (direction, direction_part, *direction_near, *direction_far),
    )
    curv, power, bound = curvature(hidden, tangent, sums, columns, F32(width), F32(total))

    quarter, f16 = depth // 4, jnp.float16

    def partial(k):
        block = lax.dynamic_slice_in_dim(gathered, ((x + k) % 4) * quarter, quarter, 1)
        return jnp.dot(curv, block, preferred_element_type=F32)

    far = partial(2).astype(f16)
    up = lax.ppermute(far[:rows], "x", shift(4, 1))
    down = lax.ppermute(far[rows:], "x", shift(4, 3))
    near_up, near_down = partial(1), partial(3)
    near_up = jnp.concatenate([near_up[:rows] + up.astype(F32), near_up[rows:]])
    near_down = jnp.concatenate([near_down[:rows], near_down[rows:] + down.astype(F32)])
    up = lax.ppermute(near_up.astype(f16), "x", shift(4, 1))
    down = lax.ppermute(near_down.astype(f16), "x", shift(4, 3))
    share = partial(0) + up.astype(F32) + down.astype(F32)

    shared = two_to(HALF_BITS - 5.0, max_z(bound)[0, 0])
    unit = jnp.exp2(-shared)
    share = share.reshape(8, rows // 4, quarter) * jnp.exp2(shared - power)
    packed = share.astype(jnp.float16)
    piece = take(share, z)
    for k in (4, 3, 5, 2, 6, 1, 7):
        piece = piece + lax.ppermute(take(packed, (z + k) % 8), Z, zshift(k)).astype(F32)

    packed = piece.astype(jnp.float16)
    line = jnp.zeros((4,) + packed.shape, jnp.float16)
    line = lax.dynamic_update_index_in_dim(line, packed, zl, 0)
    for k in (3, 1, 2):
        got = lax.ppermute(packed, "zl", shift(4, k))
        line = lax.dynamic_update_index_in_dim(line, got, (zl - k) % 4, 0)
    product = lax.all_gather(line.reshape(rows, quarter), "x", axis=0, tiled=False)
    product = product.transpose(1, 0, 2).reshape(rows, depth).astype(F32)

    scalars = jnp.stack([unit, beta_prev[0]])
    table = sums_of(scalars, product, cur, prev)
    moved = [lax.ppermute(table, ("zh", "c"), xor(4, k)) for k in (2, 3, 1)]
    table = (table + moved[2]) + (moved[0] + moved[1])
    table = table + lax.ppermute(table, "y", xor(4, 1))
    table = table + lax.ppermute(table, "y", xor(4, 3))
    fresh, coefficients = step_of(float(16 * rows * depth), scalars, table, product, cur, prev)
    return (fresh, coefficients[0, :2])


def solution(mesh):
    inner = Mesh(mesh.devices.reshape(4, 4, 4, 2, 2), ("zl", "x", "y", "zh", "c"))
    dp, shard = ("zl", "x"), ("y", "zh", "c")
    return jax.shard_map(
        per_device,
        mesh=inner,
        in_specs=(
            P(dp + shard, None),
            P(None, dp + shard),
            P(shard, None),
            P(shard, None),
            P(shard, None),
            P(),
        ),
        out_specs=(P(shard, None), P()),
        check_vma=False,
    )
```

```python
import jax
import jax.numpy as jnp
from jax import lax
from jax.experimental import pallas as pl
from jax.experimental.pallas import tpu as pltpu
from jax.sharding import Mesh, PartitionSpec as P

EPS_NORM = 1e-05
EPS_MEAN = 1e-06
PRODUCT_BOUND = 6.0 * 170.0
HALF_BITS = 15.0
Z = ("zl", "zh")
F32 = jnp.float32


def place(z):
    return (z % 4) * 2 + z // 4


def shift(n, k):
    return [(i, (i + k) % n) for i in range(n)]


def zshift(k):
    return [(place(i), place((i + k) % 8)) for i in range(8)]


def xor(n, k):
    return [(i, i ^ k) for i in range(n)]


def sum_group(v):
    v = v + lax.ppermute(v, "c", xor(2, 1))
    v = v + lax.ppermute(v, "y", xor(4, 1))
    return v + lax.ppermute(v, "y", xor(4, 3))


def max_x(v):
    for k in (1, 3):
        v = jnp.maximum(v, lax.ppermute(v, "x", xor(4, k)))
    return v


def max_z(v, steps):
    for k in steps:
        v = jnp.maximum(v, lax.ppermute(v, Z, [(place(i), place(i ^ k)) for i in range(8)]))
    return v


def two_to(bits, bound):
    return jnp.clip(bits - jnp.ceil(jnp.log2(bound)), -100.0, 100.0)


def silu_terms(normed):
    sig = jax.nn.sigmoid(normed)
    first = sig * (1.0 + normed * (1.0 - sig))
    second = sig * (1.0 - sig) * (2.0 + normed * (1.0 - 2.0 * sig))
    return (sig, first, second)


def project_kernel(place_of, *refs):
    tokens, mats, far = refs[:10], (refs[10:14], refs[14:18]), refs[18:20]
    hid, tan, sums, gathered = refs[20:24]
    left, tok, mat_sems, tok_sems, out_sems = refs[24:]
    i = pl.program_id(0)
    x, c, half = place_of[4], place_of[5], place_of[6]
    rows, depth = mats[0][0].shape
    own, quarter = tokens[0].shape[0], depth // 4

    def mat_copies():
        copies = []
        column = [pl.multiple_of(lax.rem(x + 4 - back, 4) * quarter, 128) for back in range(4)]
        for m, parts in enumerate(mats):
            own_at, other_at = [pl.multiple_of(2 * rows * m + h * rows, 16) for h in (half, 1 - half)]
            copies.append((parts[0], left.at[pl.ds(own_at, rows), :]))
            for part, back in zip(parts[1:], (0, 1, 3)):
                copies.append((part, left.at[pl.ds(other_at, rows), pl.ds(column[back], quarter)]))
            for n, part in enumerate(far):
                at = pl.multiple_of(other_at + n * (rows // 2), 16)
                source = part.at[pl.ds(m * (rows // 2), rows // 2), :]
                copies.append((source, left.at[pl.ds(at, rows // 2), pl.ds(column[2], quarter)]))
        return [pltpu.make_async_copy(f, t, mat_sems.at[n]) for n, (f, t) in enumerate(copies)]

    def tok_copies(chunk):
        mine, theirs = pl.multiple_of(c * own, 16), pl.multiple_of((1 - c) * own, 16)
        if chunk < 3:
            pairs = ((tokens[2 * chunk], mine), (tokens[2 * chunk + 1], theirs))
        else:
            pairs = ((tokens[6], mine), (tokens[7], mine + own // 2), (tokens[8], theirs), (tokens[9], theirs + own // 2))
        return [
            pltpu.make_async_copy(
                ref, tok.at[chunk, pl.ds(pl.multiple_of(at, 16), ref.shape[0]), :], tok_sems.at[2 * chunk + n]
            )
            for n, (ref, at) in enumerate(pairs)
        ]

    def out_copy(chunk):
        at = pl.multiple_of(place_of[chunk] * 2 * own, 16)
        return pltpu.make_async_copy(tok.at[chunk], gathered.at[pl.ds(at, 2 * own), :], out_sems.at[chunk])

    @pl.when(i == 0)
    def _():
        for copy in mat_copies():
            copy.start()
        for chunk in range(4):
            for copy in tok_copies(chunk):
                copy.start()
        for copy in mat_copies():
            copy.wait()

    for chunk in range(4):

        @pl.when(i == chunk)
        def _():
            for copy in tok_copies(chunk):
                copy.wait()
            out_copy(chunk).start()

    both = lax.dot_general(
        left[...], tok[i], (((1,), (1,)), ((), ())), preferred_element_type=F32
    )
    h, t = both[: 2 * rows], both[2 * rows :]
    hid[...] = h
    tan[...] = t
    sums[...] = jnp.zeros_like(sums)
    sums[0:1, :] = jnp.sum(h * h, 0, keepdims=True)
    sums[1:2, :] = jnp.sum(h * t, 0, keepdims=True)
    sums[2:3, :] = jnp.sum(t * t, 0, keepdims=True)

    @pl.when(i == 3)
    def _():
        for chunk in range(4):
            out_copy(chunk).wait()


def project(place_of, tokens, weight, direction, far):
    own, depth = tokens[0].shape
    rows = weight[0].shape[0]
    count, step = 8 * own, 2 * own
    held = pl.BlockSpec(memory_space=pl.ANY)
    out = pl.BlockSpec((2 * rows, step), lambda i, p: (0, p[i]))
    return pl.pallas_call(
        project_kernel,
        out_shape=[
            jax.ShapeDtypeStruct((2 * rows, count), F32),
            jax.ShapeDtypeStruct((2 * rows, count), F32),
            jax.ShapeDtypeStruct((4, count), F32),
            jax.ShapeDtypeStruct((count, depth), jnp.bfloat16),
        ],
        grid_spec=pltpu.PrefetchScalarGridSpec(
            num_scalar_prefetch=1,
            grid=(4,),
            in_specs=[held] * 20,
            out_specs=[out, out, pl.BlockSpec((4, step), lambda i, p: (0, p[i])), held],
            scratch_shapes=[
                pltpu.VMEM((4 * rows, depth), jnp.bfloat16),
                pltpu.VMEM((4, step, depth), jnp.bfloat16),
                pltpu.SemaphoreType.DMA((12,)),
                pltpu.SemaphoreType.DMA((10,)),
                pltpu.SemaphoreType.DMA((4,)),
            ],
        ),
        compiler_params=pltpu.CompilerParams(vmem_limit_bytes=50 * 2**20),
        cost_estimate=pl.CostEstimate(
            flops=8 * rows * depth * count, bytes_accessed=2 * depth * (2 * count + 4 * rows), transcendentals=0
        ),
    )(place_of, *tokens, *weight, *direction, *far)


def sums_kernel(scalars, product, cur, prev, out):
    unit, coeff = scalars[0], scalars[1]
    p, c = product[...] * unit, cur[...]
    w = p - coeff * prev[...]
    rows = lax.broadcasted_iota(jnp.int32, out.shape, 0)
    table = jnp.zeros(out.shape, F32)
    for i, v in enumerate((c * p, c * c, w * w, w * c)):
        table = jnp.where(rows == i, jnp.sum(v), table)

    @pl.when(pl.program_id(0) == 0)
    def _():
        out[...] = jnp.zeros_like(out)

    out[...] += table


def sums_of(scalars, product, cur, prev):
    rows, depth = cur.shape
    block = pl.BlockSpec((rows // 4, depth), lambda i: (i, 0))
    return pl.pallas_call(
        sums_kernel,
        out_shape=jax.ShapeDtypeStruct((8, 128), F32),
        grid=(4,),
        in_specs=[pl.BlockSpec(memory_space=pltpu.SMEM), block, block, block],
        out_specs=pl.BlockSpec((8, 128), lambda i: (0, 0)),
        compiler_params=pltpu.CompilerParams(vmem_limit_bytes=32 * 2**20),
    )(scalars, product, cur, prev)


def step_kernel(entries, scalars, table, product, cur, prev, fresh, coefficients):
    unit, coeff = scalars[0], scalars[1]
    t = table[...]
    dot_cp, dot_cc, dot_ww, dot_wc = (t[i : i + 1, 0:1] for i in range(4))
    alpha = dot_cp / entries
    mean_sq = (dot_ww - 2.0 * alpha * dot_wc + alpha * alpha * dot_cc) / entries
    beta = jnp.sqrt(jnp.maximum(mean_sq, 0.0) + EPS_MEAN)
    resid = product[...] * unit - alpha * cur[...] - coeff * prev[...]
    fresh[...] = resid * (1.0 / beta)
    lane = lax.broadcasted_iota(jnp.int32, coefficients.shape, 1)
    coefficients[...] = jnp.where(lane == 0, alpha, beta)


def step_of(entries, scalars, table, product, cur, prev):
    rows, depth = cur.shape
    block = pl.BlockSpec((rows // 4, depth), lambda i: (i, 0))
    small = pl.BlockSpec((8, 128), lambda i: (0, 0))
    return pl.pallas_call(
        lambda *refs: step_kernel(entries, *refs),
        out_shape=[jax.ShapeDtypeStruct((rows, depth), F32), jax.ShapeDtypeStruct((8, 128), F32)],
        grid=(4,),
        in_specs=[pl.BlockSpec(memory_space=pltpu.SMEM), small, block, block, block],
        out_specs=[block, small],
        compiler_params=pltpu.CompilerParams(vmem_limit_bytes=32 * 2**20),
    )(scalars, table, product, cur, prev)


def curvature(hidden, tangent, sums, target, width, count):
    sums = sum_group(sums)
    squares, cross = sums[0], sums[1]
    scale = lax.rsqrt(squares / width + EPS_NORM)
    bound = jnp.sum(scale * scale * jnp.sqrt(sums[2])) * (PRODUCT_BOUND / count)
    bound = max_x(jnp.full((8, 128), bound, F32))
    power = two_to(HALF_BITS - 2.0, bound[0, 0])
    scale_dot = -(scale * scale * scale) * cross / width
    normed = hidden * scale
    normed_dot = tangent * scale + hidden * scale_dot
    sig, first, second = silu_terms(normed)
    error = normed * sig - target.astype(F32)
    grad_u = error * first / count
    grad_dot = (first * first + error * second) * normed_dot / count
    sums = sum_group(
        jnp.stack([jnp.sum(grad_u * hidden, 0), jnp.sum(grad_dot * hidden + grad_u * tangent, 0)])
    )
    inner = sums[0] / width
    inner_dot = sums[1] / width
    cube = scale * scale * scale
    result = (
        scale_dot * grad_u
        + scale * grad_dot
        - 3.0 * scale * scale * scale_dot * hidden * inner
        - cube * tangent * inner
        - cube * hidden * inner_dot
    )
    return (result * jnp.exp2(power)).astype(jnp.bfloat16), power, bound


def take(stack, index):
    return lax.dynamic_index_in_dim(stack, index, 0, keepdims=False)


def beside(own, axis):
    return lax.ppermute(own, axis, shift(4, 1)), lax.ppermute(own, axis, shift(4, 3))


def opposite(back, ahead, axis):
    half = back.shape[0] // 2
    return lax.ppermute(back[:half], axis, shift(4, 1)), lax.ppermute(ahead[half:], axis, shift(4, 3))


def over_z(own, x):
    quarter = own.shape[1] // 4
    return lax.ppermute(lax.dynamic_slice_in_dim(own, x * quarter, quarter, 1), "zh", xor(2, 1))


def swap_core(v):
    return lax.ppermute(v, "c", xor(2, 1))


def per_device(tokens, targets, weight, cur, prev, beta_prev):
    x, zl, zh = (lax.axis_index(n) for n in ("x", "zl", "zh"))
    z = zh * 4 + zl
    width, own = targets.shape
    rows, depth = weight.shape
    total = own * 256

    y, core = lax.axis_index("y"), lax.axis_index("c")
    direction = cur.astype(jnp.bfloat16)
    near = beside(tokens, "y")
    weight_part = over_z(weight, x)
    weight_near = beside(weight_part, "x")
    blocks = targets.reshape(4, 2, 2, rows, own).transpose(0, 2, 1, 3, 4).reshape(8, 2 * rows, own)
    near, weight_near, direction_part, blocks = lax.optimization_barrier(
        (near, weight_near, over_z(direction, x), blocks)
    )
    far = opposite(*near, "y")
    direction_near = beside(direction_part, "x")
    far, direction_near, weight_near = lax.optimization_barrier((far, direction_near, weight_near))
    half = rows // 2
    rows_far = [
        lax.ppermute(jnp.concatenate([w[at : at + half], d[at : at + half]]), "x", shift(4, k))
        for w, d, at, k in zip(weight_near, direction_near, (0, half), (1, 3))
    ]
    pairs = [v for block in (tokens, *near) for v in (block, swap_core(block))]
    group = (*pairs, *far, *[swap_core(v) for v in far])
    blocks, last = lax.optimization_barrier((blocks, group[-1]))
    group = (*group[:-1], last)
    columns = lax.all_to_all(blocks, ("y", "c"), split_axis=0, concat_axis=2, tiled=True)
    columns = columns.reshape(2 * rows, 8 * own)

    place_of = jnp.stack([y, (y + 3) % 4, (y + 1) % 4, (y + 2) % 4, x, core, zh])
    hidden, tangent, sums, gathered = project(
        place_of,
        group,
        (weight, weight_part, *weight_near),
        (direction, direction_part, *direction_near),
        rows_far,
    )
    curv, power, bound = curvature(hidden, tangent, sums, columns, F32(width), F32(total))

    quarter, f16 = depth // 4, jnp.float16

    def partial(k):
        block = lax.dynamic_slice_in_dim(gathered, ((x + k) % 4) * quarter, quarter, 1)
        return jnp.dot(curv, block, preferred_element_type=F32)

    far = partial(2).astype(f16)
    up = lax.ppermute(far[:rows], "x", shift(4, 1))
    down = lax.ppermute(far[rows:], "x", shift(4, 3))
    near_up, near_down = partial(1), partial(3)
    near_up = jnp.concatenate([near_up[:rows] + up.astype(F32), near_up[rows:]])
    near_down = jnp.concatenate([near_down[:rows], near_down[rows:] + down.astype(F32)])
    bound = max_z(bound, (1,))
    near_up, near_down, bound = lax.optimization_barrier((near_up.astype(f16), near_down.astype(f16), bound))
    up, down = lax.ppermute(near_up, "x", shift(4, 1)), lax.ppermute(near_down, "x", shift(4, 3))
    share = partial(0) + up.astype(F32) + down.astype(F32)

    shared = two_to(HALF_BITS - 5.0, max_z(bound, (2, 4))[0, 0])
    unit = jnp.exp2(-shared)
    share = share.reshape(8, rows // 4, quarter) * jnp.exp2(shared - power)
    packed = share.astype(jnp.float16)
    piece = take(share, z)
    for k in (4, 3, 5, 2, 6, 1, 7):
        piece = piece + lax.ppermute(take(packed, (z + k) % 8), Z, zshift(k)).astype(F32)

    packed = piece.astype(jnp.float16)
    line = jnp.zeros((4,) + packed.shape, jnp.float16)
    line = lax.dynamic_update_index_in_dim(line, packed, zl, 0)
    for k in (3, 1, 2):
        got = lax.ppermute(packed, "zl", shift(4, k))
        line = lax.dynamic_update_index_in_dim(line, got, (zl - k) % 4, 0)
    product = lax.all_gather(line.reshape(rows, quarter), "x", axis=0, tiled=False)
    product = product.transpose(1, 0, 2).reshape(rows, depth).astype(F32)

    scalars = jnp.stack([unit, beta_prev[0]])
    table = sum_group(sums_of(scalars, product, cur, prev))
    table = table + lax.ppermute(table, "zh", xor(2, 1))
    fresh, coefficients = step_of(float(16 * rows * depth), scalars, table, product, cur, prev)
    return (fresh, coefficients[0, :2])


def solution(mesh):
    inner = Mesh(mesh.devices.reshape(4, 4, 4, 2, 2), ("zl", "x", "y", "zh", "c"))
    dp, shard = ("zl", "x"), ("y", "zh", "c")
    return jax.shard_map(
        per_device,
        mesh=inner,
        in_specs=(
            P(dp + shard, None),
            P(None, dp + shard),
            P(shard, None),
            P(shard, None),
            P(shard, None),
            P(),
        ),
        out_specs=(P(shard, None), P()),
        check_vma=False,
    )
```

```python
import jax
import jax.numpy as jnp
from jax import lax
from jax.experimental import pallas as pl
from jax.experimental.pallas import tpu as pltpu
from jax.sharding import Mesh, PartitionSpec as P

EPS_NORM = 1e-05
EPS_MEAN = 1e-06
PRODUCT_BOUND = 6.0 * 170.0
HALF_BITS = 15.0
Z = ("zl", "zh")
F32 = jnp.float32


def place(z):
    return (z % 4) * 2 + z // 4


def shift(n, k):
    return [(i, (i + k) % n) for i in range(n)]


def zshift(k):
    return [(place(i), place((i + k) % 8)) for i in range(8)]


def xor(n, k):
    return [(i, i ^ k) for i in range(n)]


def sum_group(v):
    v = v + lax.ppermute(v, "c", xor(2, 1))
    v = v + lax.ppermute(v, "y", xor(4, 1))
    return v + lax.ppermute(v, "y", xor(4, 3))


def max_x(v):
    for k in (1, 3):
        v = jnp.maximum(v, lax.ppermute(v, "x", xor(4, k)))
    return v


def max_z(v, steps):
    for k in steps:
        v = jnp.maximum(v, lax.ppermute(v, Z, [(place(i), place(i ^ k)) for i in range(8)]))
    return v


def two_to(bits, bound):
    return jnp.clip(bits - jnp.ceil(jnp.log2(bound)), -100.0, 100.0)


def silu_terms(normed):
    sig = jax.nn.sigmoid(normed)
    first = sig * (1.0 + normed * (1.0 - sig))
    second = sig * (1.0 - sig) * (2.0 + normed * (1.0 - 2.0 * sig))
    return (sig, first, second)


def project_kernel(place_of, *refs):
    tokens, mats, far = refs[:10], (refs[10:14], refs[14:18]), refs[18:20]
    hid, tan, sums, gathered = refs[20:24]
    left, tok, mat_sems, tok_sems, out_sems = refs[24:]
    i = pl.program_id(0)
    x, c, half = place_of[4], place_of[5], place_of[6]
    rows, depth = mats[0][0].shape
    own, quarter = tokens[0].shape[0], depth // 4

    def mat_copies():
        copies = []
        column = [pl.multiple_of(lax.rem(x + 4 - back, 4) * quarter, 128) for back in range(4)]
        for m, parts in enumerate(mats):
            own_at, other_at = [pl.multiple_of(2 * rows * m + h * rows, 16) for h in (half, 1 - half)]
            copies.append((parts[0], left.at[pl.ds(own_at, rows), :]))
            for part, back in zip(parts[1:], (0, 1, 3)):
                copies.append((part, left.at[pl.ds(other_at, rows), pl.ds(column[back], quarter)]))
            for n, part in enumerate(far):
                at = pl.multiple_of(other_at + n * (rows // 2), 16)
                source = part.at[pl.ds(m * (rows // 2), rows // 2), :]
                copies.append((source, left.at[pl.ds(at, rows // 2), pl.ds(column[2], quarter)]))
        return [pltpu.make_async_copy(f, t, mat_sems.at[n]) for n, (f, t) in enumerate(copies)]

    def tok_copies(chunk):
        mine, theirs = pl.multiple_of(c * own, 16), pl.multiple_of((1 - c) * own, 16)
        if chunk < 3:
            pairs = ((tokens[2 * chunk], mine), (tokens[2 * chunk + 1], theirs))
        else:
            pairs = ((tokens[6], mine), (tokens[7], mine + own // 2), (tokens[8], theirs), (tokens[9], theirs + own // 2))
        return [
            pltpu.make_async_copy(
                ref, tok.at[chunk, pl.ds(pl.multiple_of(at, 16), ref.shape[0]), :], tok_sems.at[2 * chunk + n]
            )
            for n, (ref, at) in enumerate(pairs)
        ]

    def out_copy(chunk):
        at = pl.multiple_of(place_of[chunk] * 2 * own, 16)
        return pltpu.make_async_copy(tok.at[chunk], gathered.at[pl.ds(at, 2 * own), :], out_sems.at[chunk])

    @pl.when(i == 0)
    def _():
        for copy in mat_copies():
            copy.start()
        for chunk in range(4):
            for copy in tok_copies(chunk):
                copy.start()
        for copy in mat_copies():
            copy.wait()

    for chunk in range(4):

        @pl.when(i == chunk)
        def _():
            for copy in tok_copies(chunk):
                copy.wait()
            out_copy(chunk).start()

    both = lax.dot_general(
        left[...], tok[i], (((1,), (1,)), ((), ())), preferred_element_type=F32
    )
    h, t = both[: 2 * rows], both[2 * rows :]
    hid[...] = h
    tan[...] = t
    sums[...] = jnp.zeros_like(sums)
    sums[0:1, :] = jnp.sum(h * h, 0, keepdims=True)
    sums[1:2, :] = jnp.sum(h * t, 0, keepdims=True)
    sums[2:3, :] = jnp.sum(t * t, 0, keepdims=True)

    @pl.when(i == 3)
    def _():
        for chunk in range(4):
            out_copy(chunk).wait()


def project(place_of, tokens, weight, direction, far):
    own, depth = tokens[0].shape
    rows = weight[0].shape[0]
    count, step = 8 * own, 2 * own
    held = pl.BlockSpec(memory_space=pl.ANY)
    out = pl.BlockSpec((2 * rows, step), lambda i, p: (0, p[i]))
    return pl.pallas_call(
        project_kernel,
        out_shape=[
            jax.ShapeDtypeStruct((2 * rows, count), F32),
            jax.ShapeDtypeStruct((2 * rows, count), F32),
            jax.ShapeDtypeStruct((4, count), F32),
            jax.ShapeDtypeStruct((count, depth), jnp.bfloat16),
        ],
        grid_spec=pltpu.PrefetchScalarGridSpec(
            num_scalar_prefetch=1,
            grid=(4,),
            in_specs=[held] * 20,
            out_specs=[out, out, pl.BlockSpec((4, step), lambda i, p: (0, p[i])), held],
            scratch_shapes=[
                pltpu.VMEM((4 * rows, depth), jnp.bfloat16),
                pltpu.VMEM((4, step, depth), jnp.bfloat16),
                pltpu.SemaphoreType.DMA((12,)),
                pltpu.SemaphoreType.DMA((10,)),
                pltpu.SemaphoreType.DMA((4,)),
            ],
        ),
        compiler_params=pltpu.CompilerParams(vmem_limit_bytes=50 * 2**20),
        cost_estimate=pl.CostEstimate(
            flops=8 * rows * depth * count, bytes_accessed=2 * depth * (2 * count + 4 * rows), transcendentals=0
        ),
    )(place_of, *tokens, *weight, *direction, *far)


def sums_kernel(scalars, product, cur, prev, out):
    unit, coeff = scalars[0], scalars[1]
    p, c = product[...] * unit, cur[...]
    w = p - coeff * prev[...]
    rows = lax.broadcasted_iota(jnp.int32, out.shape, 0)
    table = jnp.zeros(out.shape, F32)
    for i, v in enumerate((c * p, c * c, w * w, w * c)):
        table = jnp.where(rows == i, jnp.sum(v), table)

    @pl.when(pl.program_id(0) == 0)
    def _():
        out[...] = jnp.zeros_like(out)

    out[...] += table


def sums_of(scalars, product, cur, prev):
    rows, depth = cur.shape
    block = pl.BlockSpec((rows // 4, depth), lambda i: (i, 0))
    return pl.pallas_call(
        sums_kernel,
        out_shape=jax.ShapeDtypeStruct((8, 128), F32),
        grid=(4,),
        in_specs=[pl.BlockSpec(memory_space=pltpu.SMEM), block, block, block],
        out_specs=pl.BlockSpec((8, 128), lambda i: (0, 0)),
        compiler_params=pltpu.CompilerParams(vmem_limit_bytes=32 * 2**20),
    )(scalars, product, cur, prev)


def step_kernel(entries, scalars, table, product, cur, prev, fresh, coefficients):
    unit, coeff = scalars[0], scalars[1]
    t = table[...]
    dot_cp, dot_cc, dot_ww, dot_wc = (t[i : i + 1, 0:1] for i in range(4))
    alpha = dot_cp / entries
    mean_sq = (dot_ww - 2.0 * alpha * dot_wc + alpha * alpha * dot_cc) / entries
    beta = jnp.sqrt(jnp.maximum(mean_sq, 0.0) + EPS_MEAN)
    resid = product[...] * unit - alpha * cur[...] - coeff * prev[...]
    fresh[...] = resid * (1.0 / beta)
    lane = lax.broadcasted_iota(jnp.int32, coefficients.shape, 1)
    coefficients[...] = jnp.where(lane == 0, alpha, beta)


def step_of(entries, scalars, table, product, cur, prev):
    rows, depth = cur.shape
    block = pl.BlockSpec((rows // 4, depth), lambda i: (i, 0))
    small = pl.BlockSpec((8, 128), lambda i: (0, 0))
    return pl.pallas_call(
        lambda *refs: step_kernel(entries, *refs),
        out_shape=[jax.ShapeDtypeStruct((rows, depth), F32), jax.ShapeDtypeStruct((8, 128), F32)],
        grid=(4,),
        in_specs=[pl.BlockSpec(memory_space=pltpu.SMEM), small, block, block, block],
        out_specs=[block, small],
        compiler_params=pltpu.CompilerParams(vmem_limit_bytes=32 * 2**20),
    )(scalars, table, product, cur, prev)


def curvature(hidden, tangent, sums, target, width, count):
    sums = sums + lax.ppermute(sums, "c", xor(2, 1))
    sums = sums + lax.ppermute(sums, "y", xor(4, 1))
    sums, target = lax.optimization_barrier((sums, target.astype(F32)))
    sums = sums + lax.ppermute(sums, "y", xor(4, 3))
    squares, cross = sums[0], sums[1]
    scale = lax.rsqrt(squares / width + EPS_NORM)
    bound = jnp.sum(scale * scale * jnp.sqrt(sums[2])) * (PRODUCT_BOUND / count)
    bound = max_x(jnp.full((8, 128), bound, F32))
    power = two_to(HALF_BITS - 2.0, bound[0, 0])
    scale_dot = -(scale * scale * scale) * cross / width
    normed = hidden * scale
    normed_dot = tangent * scale + hidden * scale_dot
    sig, first, second = silu_terms(normed)
    error = normed * sig - target
    grad_u = error * first / count
    grad_dot = (first * first + error * second) * normed_dot / count
    sums = sum_group(
        jnp.stack([jnp.sum(grad_u * hidden, 0), jnp.sum(grad_dot * hidden + grad_u * tangent, 0)])
    )
    inner = sums[0] / width
    inner_dot = sums[1] / width
    cube = scale * scale * scale
    result = (
        scale_dot * grad_u
        + scale * grad_dot
        - 3.0 * scale * scale * scale_dot * hidden * inner
        - cube * tangent * inner
        - cube * hidden * inner_dot
    )
    return (result * jnp.exp2(power)).astype(jnp.bfloat16), power, bound


def take(stack, index):
    return lax.dynamic_index_in_dim(stack, index, 0, keepdims=False)


def beside(own, axis):
    return lax.ppermute(own, axis, shift(4, 1)), lax.ppermute(own, axis, shift(4, 3))


def over_z(own, x):
    quarter = own.shape[1] // 4
    return lax.ppermute(lax.dynamic_slice_in_dim(own, x * quarter, quarter, 1), "zh", xor(2, 1))


def swap_core(v):
    return lax.ppermute(v, "c", xor(2, 1))


def per_device(tokens, targets, weight, cur, prev, beta_prev):
    x, zl, zh = (lax.axis_index(n) for n in ("x", "zl", "zh"))
    z = zh * 4 + zl
    width, own = targets.shape
    rows, depth = weight.shape
    total = own * 256

    y, core = lax.axis_index("y"), lax.axis_index("c")
    direction = cur.astype(jnp.bfloat16)
    near = beside(tokens, "y")
    weight_part = over_z(weight, x)
    weight_near = beside(weight_part, "x")
    blocks = targets.reshape(4, 2, 2, rows, own).transpose(0, 2, 1, 3, 4).reshape(8, 2 * rows, own)
    onward = near[0][: own // 2], near[1][own // 2 :]
    near, onward, weight_near, direction_part, blocks = lax.optimization_barrier(
        (near, onward, weight_near, over_z(direction, x), blocks)
    )
    far = lax.ppermute(onward[0], "y", shift(4, 1)), lax.ppermute(onward[1], "y", shift(4, 3))
    direction_near = beside(direction_part, "x")
    far, direction_near, weight_near = lax.optimization_barrier((far, direction_near, weight_near))
    half = rows // 2
    rows_far = [
        lax.ppermute(jnp.concatenate([w[at : at + half], d[at : at + half]]), "x", shift(4, k))
        for w, d, at, k in zip(weight_near, direction_near, (0, half), (1, 3))
    ]
    pairs = [v for block in (tokens, *near) for v in (block, swap_core(block))]
    group = (*pairs, *far, *[swap_core(v) for v in far])
    blocks, last = lax.optimization_barrier((blocks, group[-1]))
    group = (*group[:-1], last)
    columns = lax.all_to_all(blocks, ("y", "c"), split_axis=0, concat_axis=2, tiled=True)
    columns = columns.reshape(2 * rows, 8 * own)

    place_of = jnp.stack([y, (y + 3) % 4, (y + 1) % 4, (y + 2) % 4, x, core, zh])
    hidden, tangent, sums, gathered = project(
        place_of,
        group,
        (weight, weight_part, *weight_near),
        (direction, direction_part, *direction_near),
        rows_far,
    )
    curv, power, bound = curvature(hidden, tangent, sums, columns, F32(width), F32(total))

    quarter, f16 = depth // 4, jnp.float16

    def partial(k):
        block = lax.dynamic_slice_in_dim(gathered, ((x + k) % 4) * quarter, quarter, 1)
        return jnp.dot(curv, block, preferred_element_type=F32)

    far = partial(2).astype(f16)
    up = lax.ppermute(far[:rows], "x", shift(4, 1))
    down = lax.ppermute(far[rows:], "x", shift(4, 3))
    near_up, near_down = partial(1), partial(3)
    near_up = jnp.concatenate([near_up[:rows] + up.astype(F32), near_up[rows:]])
    near_down = jnp.concatenate([near_down[:rows], near_down[rows:] + down.astype(F32)])
    bound = max_z(bound, (1,))
    near_up, near_down, bound = lax.optimization_barrier((near_up.astype(f16), near_down.astype(f16), bound))
    up, down = lax.ppermute(near_up, "x", shift(4, 1)), lax.ppermute(near_down, "x", shift(4, 3))
    share = partial(0) + up.astype(F32) + down.astype(F32)

    shared = two_to(HALF_BITS - 5.0, max_z(bound, (2, 4))[0, 0])
    unit = jnp.exp2(-shared)
    share = share.reshape(8, rows // 4, quarter) * jnp.exp2(shared - power)
    packed = share.astype(jnp.float16)
    piece = take(share, z)
    for k in (4, 3, 5, 2, 6, 1, 7):
        piece = piece + lax.ppermute(take(packed, (z + k) % 8), Z, zshift(k)).astype(F32)

    packed = piece.astype(jnp.float16)
    line = jnp.zeros((4,) + packed.shape, jnp.float16)
    line = lax.dynamic_update_index_in_dim(line, packed, zl, 0)
    for k in (3, 1, 2):
        got = lax.ppermute(packed, "zl", shift(4, k))
        line = lax.dynamic_update_index_in_dim(line, got, (zl - k) % 4, 0)
    product = lax.all_gather(line.reshape(rows, quarter), "x", axis=0, tiled=False)
    product = product.transpose(1, 0, 2).reshape(rows, depth).astype(F32)

    scalars = jnp.stack([unit, beta_prev[0]])
    table = sum_group(sums_of(scalars, product, cur, prev))
    table = table + lax.ppermute(table, "zh", xor(2, 1))
    fresh, coefficients = step_of(float(16 * rows * depth), scalars, table, product, cur, prev)
    return (fresh, coefficients[0, :2])


def solution(mesh):
    inner = Mesh(mesh.devices.reshape(4, 4, 4, 2, 2), ("zl", "x", "y", "zh", "c"))
    dp, shard = ("zl", "x"), ("y", "zh", "c")
    return jax.shard_map(
        per_device,
        mesh=inner,
        in_specs=(
            P(dp + shard, None),
            P(None, dp + shard),
            P(shard, None),
            P(shard, None),
            P(shard, None),
            P(),
        ),
        out_specs=(P(shard, None), P()),
        check_vma=False,
    )
```
